256 devices in a mesh: blk: 32 (over z, y_hi, core), grp: 8 (over y_lo, x).
Axes of the slice: x: 4, y: 4 (y_hi: 2, y_lo: 2; y = y_hi * 2 + y_lo), z: 8, core: 2. Of those that a mesh axis runs over, the one named last changes fastest.
Arguments:
- coeffs: bfloat16 [4096, 360, 128], P('blk', 'grp'), may hold values from -6 to 6
- vectors: float32 [4096, 16], P(('blk', 'grp')), may hold values from -6 to 6
Outputs:
- next_vectors: float32 [4096, 16], P(('blk', 'grp'))
The draws below stay inside these ranges and needn't reach their ends.
All inputs are finite; a program needn't handle non-finite values.
Results may differ from the reference program's by a relative error of at most 0.0015.
The reference program's roundings to bfloat16 on the way count: a program that leaves them out, or rounds other values in their place, can miss the bound.
Values may be sent and summed in bfloat16 or wider, within the bound.
No kernel may reach another device: no remote copies, remote signals or barrier semaphores. Data moves between devices by JAX's collectives and lax.ppermute only.
A program may use at most 64 MiB of HBM per device.

```python
import math
import jax
import jax.numpy as jnp
from jax import lax

ANGULAR = 360
RADIAL = 64
VECTORS = 16
BLOCK = 128
PARTICLES = 4096
N_BLK = 32


def draw_coeffs(key, part):
    shape = (PARTICLES, ANGULAR, 2 * RADIAL)
    block_count = PARTICLES // BLOCK
    noise_key, pattern_key = jax.random.split(key, 2)
    order = (jnp.arange(block_count, dtype=jnp.int32) + 1) % block_count
    position = order.astype(jnp.float32) / (block_count - 1)
    width_root = math.sqrt(2.0 * ANGULAR * RADIAL)
    peak = position * (math.log(ANGULAR) + 6.0)
    share = jnp.sqrt(peak / (2.5 * width_root))
    share = jnp.repeat(share, BLOCK)[:, None, None]
    pattern = jax.random.normal(pattern_key, (block_count, 1, ANGULAR, 2 * RADIAL), jnp.float32)
    pattern = jnp.broadcast_to(pattern, (block_count, BLOCK, ANGULAR, 2 * RADIAL)).reshape(shape)
    noise = jax.random.normal(noise_key, shape, jnp.float32)
    values = jnp.sqrt(1.0 - share * share) * noise + share * pattern
    return jnp.clip(values, -6.0, 6.0).astype(jnp.bfloat16)


def level_of(own_key, extent, shards, smallest, high):
    def one(axis_at, parts):
        draws = jax.random.uniform(jax.random.fold_in(jax.random.fold_in(own_key, 6), axis_at), (parts,), jnp.float32, smallest / len(shards), high / len(shards))
        return jnp.repeat(jnp.exp(draws), extent[axis_at] // parts).reshape((-1,) + (1,) * (len(extent) - axis_at - 1))

    factor_of = one(*shards[0])
    for cut in shards[1:]:
        factor_of = factor_of * one(*cut)
    return factor_of


def bell_draw(rng, extent, spread, most, cuts=(), held_as=jnp.bfloat16):
    array = jax.random.normal(rng, extent, jnp.float32) * spread
    if len(cuts) > 0:
        array = level_of(rng, extent, cuts, -0.22, 0.18) * array
    return jnp.clip(array, min=-most, max=most).astype(held_as)


def setup_inputs(seed: int = 0) -> dict:
    arg_keys = jax.random.split(jax.random.key(seed), 3)
    return {
        "coeffs": draw_coeffs(jax.random.fold_in(arg_keys[2], 71), 0),
        "vectors": bell_draw(arg_keys[1], (PARTICLES, VECTORS), 1.0, 6.0, ((0, 256),), jnp.float32),
    }


sharpness = 2.5
epsilon = 1e-06

def trig_tables():
    freq = jnp.arange(ANGULAR, dtype=jnp.int32)
    phase = (freq[:, None] * freq[None, :] % ANGULAR).astype(jnp.float32) * (2.0 * math.pi / ANGULAR)
    return (jnp.cos(phase).astype(jnp.bfloat16), (-jnp.sin(phase)).astype(jnp.bfloat16))

def reference(coeffs, vectors):
    channels = 2 * RADIAL
    values = coeffs.astype(jnp.float32)
    mean_square = lax.optimization_barrier(jnp.mean(values * values, axis=(1, 2)))
    unit_coef = (values * lax.rsqrt(mean_square + epsilon)[:, None, None]).astype(jnp.bfloat16)
    blocks = unit_coef.reshape(N_BLK, BLOCK, ANGULAR, channels)
    cos_table, sin_table = trig_tables()
    cos_wide = cos_table.astype(jnp.float32)
    sin_wide = sin_table.astype(jnp.float32)
    factor = sharpness / math.sqrt(ANGULAR * channels)
    row_ids = jnp.arange(BLOCK, dtype=jnp.int32)
    col_ids = jnp.arange(3 * BLOCK, dtype=jnp.int32)
    is_self = row_ids[:, None] == col_ids[None, :]

    def one_block(block_index):
        own_block = blocks[block_index].astype(jnp.float32)
        columns = jnp.concatenate([blocks[block_index], blocks[(block_index - 1) % N_BLK], blocks[(block_index + 1) % N_BLK]], axis=0).astype(jnp.float32)
        swapped = jnp.concatenate([-columns[..., RADIAL:], columns[..., :RADIAL]], axis=-1)
        real_part = jnp.einsum('ikc,jkc->kij', own_block, columns).astype(jnp.bfloat16)
        imag_part = jnp.einsum('ikc,jkc->kij', own_block, swapped).astype(jnp.bfloat16)
        real_part, imag_part = lax.optimization_barrier((real_part, imag_part))
        corr = jnp.einsum('kij,km->ijm', real_part.astype(jnp.float32), cos_wide)
        corr = corr + jnp.einsum('kij,km->ijm', imag_part.astype(jnp.float32), sin_wide)
        weights = lax.optimization_barrier(jnp.mean(jnp.exp(factor * corr), axis=-1))
        return jnp.where(is_self, jnp.zeros_like(weights), weights)
    affinity = lax.map(one_block, jnp.arange(N_BLK, dtype=jnp.int32))
    degree = lax.optimization_barrier(jnp.sum(affinity, axis=-1))
    inv_root = lax.rsqrt(degree)
    scaled = vectors.reshape(N_BLK, BLOCK, VECTORS) * inv_root[..., None]
    neigh = jnp.concatenate([scaled, jnp.roll(scaled, 1, axis=0), jnp.roll(scaled, -1, axis=0)], axis=1)
    image = jnp.einsum('bij,bjv->biv', affinity, neigh, precision=lax.Precision.HIGHEST)
    image = (image * inv_root[..., None] * (3.0 * BLOCK)).reshape(N_BLK * BLOCK, VECTORS)
    root_degree = jnp.sqrt(degree).reshape(N_BLK * BLOCK)
    degree_sum = jnp.sum(degree)
    projection = jnp.dot(root_degree, image, precision=lax.Precision.HIGHEST)
    deflated = image - root_degree[:, None] * (projection / degree_sum)[None, :]
    column_msq = lax.optimization_barrier(jnp.mean(deflated * deflated, axis=0))
    return deflated * lax.rsqrt(column_msq + epsilon)[None, :]
```

```python
import functools
import math

import jax
import jax.numpy as jnp
from jax import lax
from jax.experimental import pallas as pl
from jax.experimental.pallas import tpu as pltpu
from jax.sharding import PartitionSpec as P

sharpness = 2.5
epsilon = 1e-06
HIGHEST = lax.Precision.HIGHEST
VMEM_LIMIT = 48 * 1024 * 1024


def passed_along(block, axis, distance):
    devices = range(lax.axis_size(axis))
    route = [((i - distance) % len(devices), i) for i in devices]
    return lax.ppermute(block, axis, route)


def trig_columns(freq_local, group_size):
    total = freq_local * group_size
    row_ids = jnp.arange(2 * total, dtype=jnp.int32)
    freq = row_ids // 2
    angles = jnp.arange(total, dtype=jnp.int32)
    phase = (angles[:, None] * freq[None, :] % total).astype(jnp.float32) * (2.0 * math.pi / total)
    cos_part = jnp.cos(phase).astype(jnp.bfloat16)
    sin_part = (-jnp.sin(phase)).astype(jnp.bfloat16)
    return jnp.where((row_ids % 2 == 1)[None, :], sin_part, cos_part)


def iota(shape, dim):
    return lax.broadcasted_iota(jnp.int32, shape, dim)


def dot(a, b, dims):
    return lax.dot_general(a, b, (dims, ((), ())), precision=HIGHEST, preferred_element_type=jnp.float32)


def start_kernel(group_ref, coeffs_ref, vectors_ref, out_ref, sq_ref):
    step = pl.program_id(0)
    size = coeffs_ref.shape[0]
    values = coeffs_ref[...].astype(jnp.float32)
    sq_ref[pl.ds(pl.multiple_of(step * size, size), size), :] = jnp.sum(values * values, axis=1)

    @pl.when(step == pl.num_programs(0) - 1)
    def _():
        block = sq_ref.shape[0]
        rows = vectors_ref.shape[0]
        total = dot(jnp.ones((8, sq_ref.shape[1]), jnp.float32), sq_ref[...], ((1,), (1,)))
        place = iota((rows, block), 1) == iota((rows, block), 0) + rows * group_ref[0]
        placed = dot(vectors_ref[...], place.astype(jnp.float32), ((0,), (0,)))
        for d in range(out_ref.shape[0]):
            out_ref[d, 0:8, :] = total
            out_ref[d, 8 : 8 + placed.shape[0], :] = placed


def start(group_index, coeffs, vectors, group_size):
    block, freq_local, channels = coeffs.shape
    rows = 8 + vectors.shape[1]
    steps = 4
    return pl.pallas_call(
        start_kernel,
        grid_spec=pltpu.PrefetchScalarGridSpec(
            num_scalar_prefetch=1,
            grid=(steps,),
            in_specs=[
                pl.BlockSpec((block // steps, freq_local, channels), lambda s, g: (s, 0, 0)),
                pl.BlockSpec(vectors.shape, lambda s, g: (0, 0)),
            ],
            out_specs=pl.BlockSpec((group_size, rows, block), lambda s, g: (0, 0, 0)),
            scratch_shapes=[pltpu.VMEM((block, channels), jnp.float32)],
        ),
        out_shape=jax.ShapeDtypeStruct((group_size, rows, block), jnp.float32),
        compiler_params=pltpu.CompilerParams(vmem_limit_bytes=VMEM_LIMIT),
        name="start",
    )(group_index, coeffs, vectors)


def swapped(a):
    half = a.shape[1] // 2
    wide = a.astype(jnp.float32)
    turned = pltpu.roll(wide, half, 1)
    return jnp.where(iota(a.shape, 1) < half, turned, -turned).astype(a.dtype)


def upper_half(half, block):
    gap = (iota((half, block), 1) - iota((half, block), 0)) & (block - 1)
    return (gap >= 1) & (gap <= half), gap != 0


def cross_kernel(folded, a_ref, b_ref, out_ref):
    block = a_ref.shape[1]
    half = block // 2
    parts = out_ref.shape[0]
    for k in range(a_ref.shape[0]):
        a = a_ref[k]
        lhs = jnp.concatenate([a, swapped(a)], axis=0)
        pair = lax.dot_general(lhs, b_ref[k], (((1,), (1,)), ((), ())), preferred_element_type=jnp.float32)
        real, imag = pair[:block], pair[block:]
        if folded:
            top, _ = upper_half(half, block)
            real = jnp.where(top, real[:half], real[half:])
            imag = jnp.where(top, imag[:half], imag[half:])
        rows = real.shape[0] // parts
        for d in range(parts):
            both = jnp.concatenate([real[d * rows : (d + 1) * rows], imag[d * rows : (d + 1) * rows]], axis=0)
            out_ref[d, k * 2 * rows : (k + 1) * 2 * rows, :] = both.astype(jnp.bfloat16)


def cross(folded, own, other, parts, steps):
    freq, block, channels = own.shape
    rows = freq * (block if folded else 2 * block) // parts
    one = freq // steps
    spec = pl.BlockSpec((one, block, channels), lambda s: (s, 0, 0))
    return pl.pallas_call(
        functools.partial(cross_kernel, folded),
        grid=(steps,),
        in_specs=[spec, spec],
        out_specs=pl.BlockSpec((parts, rows // steps, block), lambda s: (0, s, 0)),
        out_shape=jax.ShapeDtypeStruct((parts, rows, block), jnp.bfloat16),
        compiler_params=pltpu.CompilerParams(vmem_limit_bytes=VMEM_LIMIT),
        name="cross_own" if folded else "cross_next",
    )(own, other)


def affinities(terms_ref, trig_ref, held_ref, rows, factor):
    depth = trig_ref.shape[1]
    angles = trig_ref.shape[0]
    width = terms_ref.shape[1]
    chunk = 16 * rows
    at = iota((chunk, chunk), 0)
    turn = (iota((chunk, chunk), 1) == (at & 15) * rows + (at >> 4)).astype(jnp.bfloat16)
    for c in range(depth // 16):
        piece = terms_ref[c * chunk : (c + 1) * chunk, :]
        turned = jnp.dot(turn, piece, preferred_element_type=jnp.float32).astype(jnp.bfloat16)
        for i in range(rows):
            held_ref[c * 16 : (c + 1) * 16, i * width : (i + 1) * width] = turned[i * 16 : (i + 1) * 16]
    out = []
    for pair in range(rows // 2):
        corr = jnp.dot(
            trig_ref[...], held_ref[:, pair * 2 * width : (pair + 1) * 2 * width], preferred_element_type=jnp.float32
        )
        mean = jnp.sum(jnp.exp(factor * corr), axis=0, keepdims=True) * (1.0 / angles)
        out += [mean[:, :width], mean[:, width:]]
    return out


def own_kernel(factor, group_ref, terms_ref, trig_ref, out_ref, held_ref):
    rows = 8
    block = terms_ref.shape[1]
    means = affinities(terms_ref, trig_ref, held_ref, rows, factor)
    for i in range(rows):
        out_ref[i : i + 1, :] = means[i]
    at = iota((rows, block), 0) + rows * group_ref[0]
    gap = (iota((rows, block), 1) - at) & (block - 1)
    out_ref[...] = jnp.where(gap == 0, 0.0, out_ref[...])


def own_part(group_index, terms, trig, factor):
    rows = 8
    block = terms.shape[1]
    return pl.pallas_call(
        functools.partial(own_kernel, factor),
        in_specs=[pl.BlockSpec(memory_space=pltpu.SMEM)] + [pl.BlockSpec(memory_space=pltpu.VMEM)] * 2,
        out_specs=pl.BlockSpec(memory_space=pltpu.VMEM),
        out_shape=jax.ShapeDtypeStruct((rows, block), jnp.float32),
        scratch_shapes=[pltpu.VMEM((trig.shape[1], rows * block), jnp.bfloat16)],
        compiler_params=pltpu.CompilerParams(vmem_limit_bytes=VMEM_LIMIT),
        name="own_part",
    )(group_index, terms, trig)


def next_kernel(factor, group_ref, terms_ref, trig_ref, own_ref, out_ref, held_ref, wide_ref):
    rows = 16
    block = terms_ref.shape[1]
    half = block // 2
    group = group_ref[0]
    means = affinities(terms_ref, trig_ref, held_ref, rows, factor)
    for i in range(rows):
        out_ref[i : i + 1, :] = means[i]
    own = own_ref[...]
    at = iota((8, block), 0) + 8 * group
    gap = (iota((8, block), 1) - at) & (block - 1)
    top = (gap >= 1) & (gap <= half)
    upper, lower = jnp.where(top, own, 0.0), jnp.where(top, 0.0, own)
    wide_ref[...] = jnp.zeros_like(wide_ref)
    wide_ref[pl.ds(pl.multiple_of(rows * group, rows), rows), :] = out_ref[0:rows, :]
    own_at = pl.multiple_of(8 * group, 8)
    wide_ref[pl.ds(block + own_at, 8), :] = upper
    wide_ref[pl.ds(block + half + own_at, 8), :] = lower
    ones = jnp.ones((8, block), jnp.float32)
    by_row = dot(ones, wide_ref[...], ((1,), (1,)))
    degree = by_row[0:1, :block] + by_row[0:1, block:] + jnp.sum(own, axis=0, keepdims=True)
    out_ref[rows : rows + 8, :] = jnp.zeros((8, block), jnp.float32)
    out_ref[rows : rows + 1, :] = degree
    out_ref[rows + 1 : rows + 2, :] = jnp.sum(out_ref[0:rows, :], axis=0, keepdims=True)


def next_part(group_index, terms, trig, own, factor):
    rows = 16
    block = terms.shape[1]
    return pl.pallas_call(
        functools.partial(next_kernel, factor),
        in_specs=[pl.BlockSpec(memory_space=pltpu.SMEM)] + [pl.BlockSpec(memory_space=pltpu.VMEM)] * 3,
        out_specs=pl.BlockSpec(memory_space=pltpu.VMEM),
        out_shape=jax.ShapeDtypeStruct((rows + 8, block), jnp.float32),
        scratch_shapes=[
            pltpu.VMEM((trig.shape[1], rows * block), jnp.bfloat16),
            pltpu.VMEM((2 * block, block), jnp.float32),
        ],
        compiler_params=pltpu.CompilerParams(vmem_limit_bytes=VMEM_LIMIT),
        name="next_part",
    )(group_index, terms, trig, own)


def image_kernel(group_ref, parts_ref, vec_ref, out_ref, own_ref, full_ref):
    groups, _, block = parts_ref.shape
    half = block // 2
    shares = parts_ref[0, 40:48, :]
    for s in range(groups):
        if s:
            shares = shares + parts_ref[s, 40:48, :]
        full_ref[0, 16 * s : 16 * s + 16, :] = parts_ref[s, 0:16, :]
        full_ref[1, 16 * s : 16 * s + 16, :] = parts_ref[s, 16:32, :]
        full_ref[2, 8 * s : 8 * s + 8, :] = parts_ref[s, 32:40, :]
    top, _ = upper_half(half, block)
    own = full_ref[2, 0:half, :]
    full_ref[2, 0:half, :] = jnp.where(top, own, 0.0)
    full_ref[2, half:block, :] = jnp.where(top, 0.0, own)
    inv_root = lax.rsqrt(shares)
    scaled_before = vec_ref[0] * inv_root[0:1, :]
    scaled_own = vec_ref[1] * inv_root[1:2, :]
    scaled_after = vec_ref[2] * inv_root[2:3, :]
    along, across = ((1,), (1,)), ((1,), (0,))
    product = dot(scaled_own, full_ref[2], along) + dot(scaled_own, full_ref[2], across)
    product = product + dot(scaled_after, full_ref[0], along) + dot(scaled_before, full_ref[1], across)
    image = product * inv_root[1:2, :] * (3.0 * block)
    degree = shares[1:2, :]
    root_degree = jnp.sqrt(degree)
    degree_sum = jnp.sum(degree, axis=1, keepdims=True)
    proj = jnp.sum(root_degree * image, axis=1, keepdims=True)
    rest = image - root_degree * (proj / degree_sum)
    rest_sq = jnp.sum(rest * rest, axis=1, keepdims=True)
    count = image.shape[0]
    at, lane = iota((count, block), 0), iota((count, block), 1)
    stats = jnp.where(lane == at, proj, 0.0) + jnp.where(lane == at + count, rest_sq, 0.0)
    stats = jnp.sum(stats, axis=0, keepdims=True)
    stats = jnp.where(iota((1, block), 1) == 2 * count, degree_sum, stats)
    out_ref[...] = jnp.broadcast_to(stats, out_ref.shape)
    place = (lane == at + count * group_ref[0]).astype(jnp.float32)
    own_ref[0] = dot(place, image, along)
    own_ref[1] = dot(place, jnp.broadcast_to(root_degree, image.shape), along)


def image_part(group_index, parts, vecs, n_blk):
    groups, _, block = parts.shape
    count = vecs.shape[1]
    return pl.pallas_call(
        image_kernel,
        in_specs=[pl.BlockSpec(memory_space=pltpu.SMEM)] + [pl.BlockSpec(memory_space=pltpu.VMEM)] * 2,
        out_specs=[pl.BlockSpec(memory_space=pltpu.VMEM)] * 2,
        out_shape=[
            jax.ShapeDtypeStruct((n_blk, block), jnp.float32),
            jax.ShapeDtypeStruct((2, count, count), jnp.float32),
        ],
        scratch_shapes=[pltpu.VMEM((3, block, block), jnp.float32)],
        compiler_params=pltpu.CompilerParams(vmem_limit_bytes=VMEM_LIMIT),
        name="image_part",
    )(group_index, parts, vecs)


def final_kernel(total_rows, stats_ref, own_ref, out_ref):
    count = out_ref.shape[1]
    stats = stats_ref[...]
    proj, rest_sq, degree = stats[:, :count], stats[:, count : 2 * count], stats[:, 2 * count : 2 * count + 1]
    ratio = jnp.sum(proj, axis=0, keepdims=True) / jnp.sum(degree, axis=0, keepdims=True)
    shift = proj / degree - ratio
    column_sq = jnp.sum(rest_sq + degree * (shift * shift), axis=0, keepdims=True)
    deflated = own_ref[0] - own_ref[1] * ratio
    out_ref[...] = deflated * lax.rsqrt(column_sq / total_rows + epsilon)


def final_part(stats, own, total_rows):
    count = own.shape[1]
    return pl.pallas_call(
        functools.partial(final_kernel, total_rows),
        in_specs=[pl.BlockSpec(memory_space=pltpu.VMEM)] * 2,
        out_specs=pl.BlockSpec(memory_space=pltpu.VMEM),
        out_shape=jax.ShapeDtypeStruct((count, count), jnp.float32),
        name="final_part",
    )(stats, own)


def per_device(coeffs, vectors):
    block, freq_local, channels = coeffs.shape
    group_size = lax.axis_size("grp")
    n_blk = lax.axis_size("blk")
    group_index = lax.axis_index("grp").astype(jnp.int32)[None]
    angles = freq_local * group_size
    factor = sharpness / math.sqrt(angles * channels)
    trig = trig_columns(freq_local, group_size)

    after_raw = passed_along(coeffs, "blk", -1)
    begun = start(group_index, coeffs, vectors, group_size)
    summed = jnp.sum(lax.all_to_all(begun, "grp", 0, 0, tiled=True), axis=0)
    summed_after = passed_along(summed, "blk", -1)
    summed_before = passed_along(summed, "blk", 1)

    def unit(raw, sums):
        inv_norm = lax.rsqrt(sums[0] / (angles * channels) + epsilon)
        return (raw.astype(jnp.float32) * inv_norm[:, None, None]).astype(jnp.bfloat16).transpose(1, 0, 2)

    own_unit = unit(coeffs, summed)
    own_terms = cross(True, own_unit, own_unit, group_size, 5)
    own_terms = lax.all_to_all(own_terms, "grp", 0, 0, tiled=True).reshape(-1, block)
    after_unit = unit(after_raw, summed_after)
    next_terms = cross(False, own_unit, after_unit, group_size, 5)
    next_terms = lax.all_to_all(next_terms, "grp", 0, 0, tiled=True).reshape(-1, block)
    own_aff = own_part(group_index, own_terms, trig, factor)
    found = next_part(group_index, next_terms, trig, own_aff, factor)

    found_before = passed_along(found, "blk", 1)
    edge_after = passed_along(found[16:], "blk", -1)
    edge_before = passed_along(found[16:], "blk", 2)
    zeros = jnp.zeros((5, block), jnp.float32)
    shares = jnp.concatenate(
        [
            found_before[16:17] + edge_before[1:2],
            found[16:17] + found_before[17:18],
            edge_after[0:1] + found[17:18],
            zeros,
        ],
        axis=0,
    )
    sent = jnp.concatenate([found[:16], found_before[:16], own_aff, shares], axis=0)
    sent = jnp.broadcast_to(sent[None], (group_size,) + sent.shape)
    parts = lax.all_to_all(sent, "grp", 0, 0, tiled=True)
    vecs = jnp.stack([summed_before[8:], summed[8:], summed_after[8:]])
    stats, own = image_part(group_index, parts, vecs, n_blk)
    stats = lax.all_to_all(stats, "blk", 0, 0, tiled=True)
    return final_part(stats, own, block * n_blk)


def solution(mesh):
    placed = (P("blk", "grp", None), P(("blk", "grp"), None))
    return jax.shard_map(
        per_device, mesh=mesh, in_specs=placed, out_specs=P(("blk", "grp"), None), check_vma=False
    )
```

```python
import functools
import math

import jax
import jax.numpy as jnp
from jax import lax
from jax.experimental import pallas as pl
from jax.experimental.pallas import tpu as pltpu
from jax.sharding import PartitionSpec as P

sharpness = 2.5
epsilon = 1e-06
HIGHEST = lax.Precision.HIGHEST
VMEM_LIMIT = 48 * 1024 * 1024


def passed_along(block, axis, distance):
    devices = range(lax.axis_size(axis))
    route = [((i - distance) % len(devices), i) for i in devices]
    return lax.ppermute(block, axis, route)


def trig_columns(freq_local, group_size):
    total = freq_local * group_size
    row_ids = jnp.arange(2 * total, dtype=jnp.int32)
    freq = row_ids // 2
    angles = jnp.arange(total, dtype=jnp.int32)
    phase = (angles[:, None] * freq[None, :] % total).astype(jnp.float32) * (2.0 * math.pi / total)
    cos_part = jnp.cos(phase).astype(jnp.bfloat16)
    sin_part = (-jnp.sin(phase)).astype(jnp.bfloat16)
    return jnp.where((row_ids % 2 == 1)[None, :], sin_part, cos_part)


def iota(shape, dim):
    return lax.broadcasted_iota(jnp.int32, shape, dim)


def dot(a, b, dims):
    return lax.dot_general(a, b, (dims, ((), ())), precision=HIGHEST, preferred_element_type=jnp.float32)


def start_kernel(group_ref, coeffs_ref, vectors_ref, out_ref, sq_ref):
    step = pl.program_id(0)

    @pl.when(step == 0)
    def _():
        sq_ref[...] = jnp.zeros_like(sq_ref)

    total = sq_ref[...]
    for k in range(coeffs_ref.shape[0]):
        values = coeffs_ref[k].astype(jnp.float32)
        total = total + values * values
    sq_ref[...] = total

    @pl.when(step == pl.num_programs(0) - 1)
    def _():
        block = sq_ref.shape[0]
        rows = vectors_ref.shape[0]
        total = dot(jnp.ones((8, sq_ref.shape[1]), jnp.float32), sq_ref[...], ((1,), (1,)))
        place = iota((rows, block), 1) == iota((rows, block), 0) + rows * group_ref[0]
        placed = dot(vectors_ref[...], place.astype(jnp.float32), ((0,), (0,)))
        for d in range(out_ref.shape[0]):
            out_ref[d, 0:8, :] = total
            out_ref[d, 8 : 8 + placed.shape[0], :] = placed


def start(group_index, coeffs, vectors, group_size):
    freq_local, block, channels = coeffs.shape
    rows = 8 + vectors.shape[1]
    steps = 5
    return pl.pallas_call(
        start_kernel,
        grid_spec=pltpu.PrefetchScalarGridSpec(
            num_scalar_prefetch=1,
            grid=(steps,),
            in_specs=[
                pl.BlockSpec((freq_local // steps, block, channels), lambda s, g: (s, 0, 0)),
                pl.BlockSpec(vectors.shape, lambda s, g: (0, 0)),
            ],
            out_specs=pl.BlockSpec((group_size, rows, block), lambda s, g: (0, 0, 0)),
            scratch_shapes=[pltpu.VMEM((block, channels), jnp.float32)],
        ),
        out_shape=pltpu.HBM((group_size, rows, block), jnp.float32),
        compiler_params=pltpu.CompilerParams(vmem_limit_bytes=VMEM_LIMIT),
        name="start",
    )(group_index, coeffs, vectors)


def swapped(a):
    half = a.shape[1] // 2
    wide = a.astype(jnp.float32)
    turned = pltpu.roll(wide, half, 1)
    return jnp.where(iota(a.shape, 1) < half, turned, -turned).astype(a.dtype)


def upper_half(half, block):
    gap = (iota((half, block), 1) - iota((half, block), 0)) & (block - 1)
    return (gap >= 1) & (gap <= half)


def inverse_norm(total, count):
    block = total.shape[1]
    eye = iota((block, block), 0) == iota((block, block), 1)
    column = jnp.sum(jnp.where(eye, total, 0.0), axis=1, keepdims=True)
    return lax.rsqrt(column / count + epsilon)


def normalized(raw, inv_norm):
    return (raw.astype(jnp.float32) * inv_norm).astype(jnp.bfloat16)


def pair_terms(own, other):
    lhs = jnp.concatenate([own, swapped(own)], axis=0)
    pair = lax.dot_general(lhs, other, (((1,), (1,)), ((), ())), preferred_element_type=jnp.float32)
    return pair[: own.shape[0]], pair[own.shape[0] :]


def store_terms(out_ref, k, real, imag):
    parts = out_ref.shape[0]
    rows = real.shape[0] // parts
    for d in range(parts):
        both = jnp.concatenate([real[d * rows : (d + 1) * rows], imag[d * rows : (d + 1) * rows]], axis=0)
        out_ref[d, k * 2 * rows : (k + 1) * 2 * rows, :] = both.astype(jnp.bfloat16)


def cross_own_kernel(count, raw_ref, begun_ref, out_ref, unit_ref, summed_ref, inv_ref):
    block = raw_ref.shape[1]
    half = block // 2

    @pl.when(pl.program_id(0) == 0)
    def _():
        summed_ref[...] = jnp.sum(begun_ref[...], axis=0)
        inv_ref[...] = jnp.broadcast_to(inverse_norm(summed_ref[0:1, :], count), inv_ref.shape)

    inv_norm = inv_ref[...]
    top = upper_half(half, block)
    for k in range(raw_ref.shape[0]):
        unit = normalized(raw_ref[k], inv_norm)
        unit_ref[k] = unit
        real, imag = pair_terms(unit, unit)
        store_terms(out_ref, k, jnp.where(top, real[:half], real[half:]), jnp.where(top, imag[:half], imag[half:]))


def cross_own(raw, begun, steps):
    freq, block, channels = raw.shape
    parts, sums, _ = begun.shape
    rows = freq * block // parts
    spec = pl.BlockSpec((freq // steps, block, channels), lambda s: (s, 0, 0))
    return pl.pallas_call(
        functools.partial(cross_own_kernel, freq * parts * channels),
        grid=(steps,),
        in_specs=[spec, pl.BlockSpec(begun.shape, lambda s: (0, 0, 0))],
        out_specs=[
            pl.BlockSpec((parts, rows // steps, block), lambda s: (0, s, 0)),
            spec,
            pl.BlockSpec((sums, block), lambda s: (0, 0)),
        ],
        out_shape=[
            pltpu.HBM((parts, rows, block), jnp.bfloat16),
            pltpu.HBM(raw.shape, jnp.bfloat16),
            jax.ShapeDtypeStruct((sums, block), jnp.float32),
        ],
        scratch_shapes=[pltpu.VMEM((block, channels), jnp.float32)],
        compiler_params=pltpu.CompilerParams(vmem_limit_bytes=VMEM_LIMIT),
        name="cross_own",
    )(raw, begun)


def cross_next_kernel(count, unit_ref, raw_ref, summed_ref, out_ref, inv_ref):
    @pl.when(pl.program_id(0) == 0)
    def _():
        inv_ref[...] = jnp.broadcast_to(inverse_norm(summed_ref[0:1, :], count), inv_ref.shape)

    inv_norm = inv_ref[...]
    for k in range(raw_ref.shape[0]):
        real, imag = pair_terms(unit_ref[k], normalized(raw_ref[k], inv_norm))
        store_terms(out_ref, k, real, imag)


def cross_next(unit, raw, summed, parts, steps):
    freq, block, channels = raw.shape
    rows = freq * 2 * block // parts
    spec = pl.BlockSpec((freq // steps, block, channels), lambda s: (s, 0, 0))
    return pl.pallas_call(
        functools.partial(cross_next_kernel, freq * parts * channels),
        grid=(steps,),
        in_specs=[spec, spec, pl.BlockSpec(summed.shape, lambda s: (0, 0))],
        out_specs=pl.BlockSpec((parts, rows // steps, block), lambda s: (0, s, 0)),
        out_shape=pltpu.HBM((parts, rows, block), jnp.bfloat16),
        scratch_shapes=[pltpu.VMEM((block, channels), jnp.float32)],
        compiler_params=pltpu.CompilerParams(vmem_limit_bytes=VMEM_LIMIT),
        name="cross_next",
    )(unit, raw, summed)


def affinities(terms_ref, trig_ref, held_ref, rows, factor):
    depth = trig_ref.shape[1]
    angles = trig_ref.shape[0]
    width = terms_ref.shape[1]
    chunk = 16 * rows
    at = iota((chunk, chunk), 0)
    turn = (iota((chunk, chunk), 1) == (at & 15) * rows + (at >> 4)).astype(jnp.bfloat16)
    for c in range(depth // 16):
        piece = terms_ref[c * chunk : (c + 1) * chunk, :]
        turned = jnp.dot(turn, piece, preferred_element_type=jnp.float32).astype(jnp.bfloat16)
        for i in range(rows):
            held_ref[c * 16 : (c + 1) * 16, i * width : (i + 1) * width] = turned[i * 16 : (i + 1) * 16]
    out = []
    for pair in range(rows // 2):
        corr = jnp.dot(
            trig_ref[...], held_ref[:, pair * 2 * width : (pair + 1) * 2 * width], preferred_element_type=jnp.float32
        )
        mean = jnp.sum(jnp.exp(factor * corr), axis=0, keepdims=True) * (1.0 / angles)
        out += [mean[:, :width], mean[:, width:]]
    return out


def own_kernel(factor, group_ref, far_ref, trig_ref, out_ref, held_ref, terms_ref, sem):
    rows = 8
    block = terms_ref.shape[1]
    fetch = pltpu.make_async_copy(far_ref, terms_ref, sem)
    fetch.start()
    fetch.wait()
    means = affinities(terms_ref, trig_ref, held_ref, rows, factor)
    for i in range(rows):
        out_ref[i : i + 1, :] = means[i]
    at = iota((rows, block), 0) + rows * group_ref[0]
    gap = (iota((rows, block), 1) - at) & (block - 1)
    out_ref[...] = jnp.where(gap == 0, 0.0, out_ref[...])


def own_part(group_index, terms, trig, factor):
    rows = 8
    block = terms.shape[1]
    return pl.pallas_call(
        functools.partial(own_kernel, factor),
        in_specs=[
            pl.BlockSpec(memory_space=pltpu.SMEM),
            pl.BlockSpec(memory_space=pltpu.HBM),
            pl.BlockSpec(memory_space=pltpu.VMEM),
        ],
        out_specs=pl.BlockSpec(memory_space=pltpu.VMEM),
        out_shape=jax.ShapeDtypeStruct((rows, block), jnp.float32),
        scratch_shapes=[
            pltpu.VMEM((trig.shape[1], rows * block), jnp.bfloat16),
            pltpu.VMEM(terms.shape, terms.dtype),
            pltpu.SemaphoreType.DMA,
        ],
        compiler_params=pltpu.CompilerParams(vmem_limit_bytes=VMEM_LIMIT),
        name="own_part",
    )(group_index, terms, trig)


def next_kernel(factor, group_ref, terms_ref, trig_ref, own_ref, out_ref, held_ref, wide_ref):
    rows = 16
    block = terms_ref.shape[1]
    half = block // 2
    group = group_ref[0]
    means = affinities(terms_ref, trig_ref, held_ref, rows, factor)
    for i in range(rows):
        out_ref[i : i + 1, :] = means[i]
    own = own_ref[...]
    at = iota((8, block), 0) + 8 * group
    gap = (iota((8, block), 1) - at) & (block - 1)
    top = (gap >= 1) & (gap <= half)
    upper, lower = jnp.where(top, own, 0.0), jnp.where(top, 0.0, own)
    wide_ref[...] = jnp.zeros_like(wide_ref)
    wide_ref[pl.ds(pl.multiple_of(rows * group, rows), rows), :] = out_ref[0:rows, :]
    own_at = pl.multiple_of(8 * group, 8)
    wide_ref[pl.ds(block + own_at, 8), :] = upper
    wide_ref[pl.ds(block + half + own_at, 8), :] = lower
    ones = jnp.ones((8, block), jnp.float32)
    by_row = dot(ones, wide_ref[...], ((1,), (1,)))
    degree = by_row[0:1, :block] + by_row[0:1, block:] + jnp.sum(own, axis=0, keepdims=True)
    out_ref[rows : rows + 8, :] = jnp.zeros((8, block), jnp.float32)
    out_ref[rows : rows + 1, :] = degree
    out_ref[rows + 1 : rows + 2, :] = jnp.sum(out_ref[0:rows, :], axis=0, keepdims=True)


def next_part(group_index, terms, trig, own, factor):
    rows = 16
    block = terms.shape[1]
    return pl.pallas_call(
        functools.partial(next_kernel, factor),
        in_specs=[pl.BlockSpec(memory_space=pltpu.SMEM)] + [pl.BlockSpec(memory_space=pltpu.VMEM)] * 3,
        out_specs=pl.BlockSpec(memory_space=pltpu.VMEM),
        out_shape=jax.ShapeDtypeStruct((rows + 8, block), jnp.float32),
        scratch_shapes=[
            pltpu.VMEM((trig.shape[1], rows * block), jnp.bfloat16),
            pltpu.VMEM((2 * block, block), jnp.float32),
        ],
        compiler_params=pltpu.CompilerParams(vmem_limit_bytes=VMEM_LIMIT),
        name="next_part",
    )(group_index, terms, trig, own)


def image_kernel(group_ref, parts_ref, before_ref, here_ref, after_ref, out_ref, own_ref, full_ref):
    groups, _, block = parts_ref.shape
    half = block // 2
    shares = parts_ref[0, 40:48, :]
    for s in range(groups):
        if s:
            shares = shares + parts_ref[s, 40:48, :]
        full_ref[0, 16 * s : 16 * s + 16, :] = parts_ref[s, 0:16, :]
        full_ref[1, 16 * s : 16 * s + 16, :] = parts_ref[s, 16:32, :]
        full_ref[2, 8 * s : 8 * s + 8, :] = parts_ref[s, 32:40, :]
    top = upper_half(half, block)
    own = full_ref[2, 0:half, :]
    full_ref[2, 0:half, :] = jnp.where(top, own, 0.0)
    full_ref[2, half:block, :] = jnp.where(top, 0.0, own)
    inv_root = lax.rsqrt(shares)
    scaled_before = before_ref[8:, :] * inv_root[0:1, :]
    scaled_own = here_ref[8:, :] * inv_root[1:2, :]
    scaled_after = after_ref[8:, :] * inv_root[2:3, :]
    along, across = ((1,), (1,)), ((1,), (0,))
    product = dot(scaled_own, full_ref[2], along) + dot(scaled_own, full_ref[2], across)
    product = product + dot(scaled_after, full_ref[0], along) + dot(scaled_before, full_ref[1], across)
    image = product * inv_root[1:2, :] * (3.0 * block)
    degree = shares[1:2, :]
    root_degree = jnp.sqrt(degree)
    degree_sum = jnp.sum(degree, axis=1, keepdims=True)
    proj = jnp.sum(root_degree * image, axis=1, keepdims=True)
    rest = image - root_degree * (proj / degree_sum)
    rest_sq = jnp.sum(rest * rest, axis=1, keepdims=True)
    count = image.shape[0]
    at, lane = iota((count, block), 0), iota((count, block), 1)
    stats = jnp.where(lane == at, proj, 0.0) + jnp.where(lane == at + count, rest_sq, 0.0)
    stats = jnp.sum(stats, axis=0, keepdims=True)
    stats = jnp.where(iota((1, block), 1) == 2 * count, degree_sum, stats)
    out_ref[...] = jnp.broadcast_to(stats, out_ref.shape)
    place = (lane == at + count * group_ref[0]).astype(jnp.float32)
    own_ref[0] = dot(place, image, along)
    own_ref[1] = dot(place, jnp.broadcast_to(root_degree, image.shape), along)


def image_part(group_index, parts, before, here, after, n_blk):
    groups, _, block = parts.shape
    count = here.shape[0] - 8
    return pl.pallas_call(
        image_kernel,
        in_specs=[pl.BlockSpec(memory_space=pltpu.SMEM)] + [pl.BlockSpec(memory_space=pltpu.VMEM)] * 4,
        out_specs=[pl.BlockSpec(memory_space=pltpu.VMEM)] * 2,
        out_shape=[
            jax.ShapeDtypeStruct((n_blk, block), jnp.float32),
            jax.ShapeDtypeStruct((2, count, count), jnp.float32),
        ],
        scratch_shapes=[pltpu.VMEM((3, block, block), jnp.float32)],
        compiler_params=pltpu.CompilerParams(vmem_limit_bytes=VMEM_LIMIT),
        name="image_part",
    )(group_index, parts, before, here, after)


def final_kernel(total_rows, stats_ref, own_ref, out_ref):
    count = out_ref.shape[1]
    stats = stats_ref[...]
    proj, rest_sq, degree = stats[:, :count], stats[:, count : 2 * count], stats[:, 2 * count : 2 * count + 1]
    ratio = jnp.sum(proj, axis=0, keepdims=True) / jnp.sum(degree, axis=0, keepdims=True)
    shift = proj / degree - ratio
    column_sq = jnp.sum(rest_sq + degree * (shift * shift), axis=0, keepdims=True)
    deflated = own_ref[0] - own_ref[1] * ratio
    out_ref[...] = deflated * lax.rsqrt(column_sq / total_rows + epsilon)


def final_part(stats, own, total_rows):
    count = own.shape[1]
    return pl.pallas_call(
        functools.partial(final_kernel, total_rows),
        in_specs=[pl.BlockSpec(memory_space=pltpu.VMEM)] * 2,
        out_specs=pl.BlockSpec(memory_space=pltpu.VMEM),
        out_shape=jax.ShapeDtypeStruct((count, count), jnp.float32),
        name="final_part",
    )(stats, own)


def per_device(coeffs, vectors):
    block, freq_local, channels = coeffs.shape
    group_size = lax.axis_size("grp")
    n_blk = lax.axis_size("blk")
    group_index = lax.axis_index("grp").astype(jnp.int32)[None]
    angles = freq_local * group_size
    factor = sharpness / math.sqrt(angles * channels)
    trig = trig_columns(freq_local, group_size)

    by_freq = coeffs.transpose(1, 0, 2)
    after_raw = passed_along(by_freq, "blk", -1)
    begun = lax.all_to_all(start(group_index, by_freq, vectors, group_size), "grp", 0, 0, tiled=True)
    own_terms, own_unit, summed = cross_own(by_freq, begun, 5)
    own_terms = lax.all_to_all(own_terms, "grp", 0, 0, tiled=True).reshape(-1, block)
    summed_after = passed_along(summed, "blk", -1)
    summed_before = passed_along(summed, "blk", 1)
    next_terms = cross_next(own_unit, after_raw, summed_after, group_size, 5)
    next_terms = lax.all_to_all(next_terms, "grp", 0, 0, tiled=True).reshape(-1, block)
    own_aff = own_part(group_index, own_terms, trig, factor)
    found = next_part(group_index, next_terms, trig, own_aff, factor)

    found_before = passed_along(found, "blk", 1)
    edge_after = passed_along(found[16:], "blk", -1)
    edge_before = passed_along(found[16:], "blk", 2)
    zeros = jnp.zeros((5, block), jnp.float32)
    shares = jnp.concatenate(
        [
            found_before[16:17] + edge_before[1:2],
            found[16:17] + found_before[17:18],
            edge_after[0:1] + found[17:18],
            zeros,
        ],
        axis=0,
    )
    sent = jnp.concatenate([found[:16], found_before[:16], own_aff, shares], axis=0)
    sent = jnp.broadcast_to(sent[None], (group_size,) + sent.shape)
    parts = lax.all_to_all(sent, "grp", 0, 0, tiled=True)
    stats, own = image_part(group_index, parts, summed_before, summed, summed_after, n_blk)
    stats = lax.all_to_all(stats, "blk", 0, 0, tiled=True)
    return final_part(stats, own, block * n_blk)


def solution(mesh):
    placed = (P("blk", "grp", None), P(("blk", "grp"), None))
    return jax.shard_map(
        per_device, mesh=mesh, in_specs=placed, out_specs=P(("blk", "grp"), None), check_vma=False
    )
```

```python
import functools
import math

import jax
import jax.numpy as jnp
from jax import lax
from jax.experimental import pallas as pl
from jax.experimental.pallas import tpu as pltpu
from jax.sharding import PartitionSpec as P

sharpness = 2.5
epsilon = 1e-06
HIGHEST = lax.Precision.HIGHEST
VMEM_LIMIT = 48 * 1024 * 1024


def passed_along(block, axis, distance):
    devices = range(lax.axis_size(axis))
    route = [((i - distance) % len(devices), i) for i in devices]
    return lax.ppermute(block, axis, route)


def trig_columns(freq_local, group_size, group_index):
    total = freq_local * group_size
    row_ids = jnp.arange(2 * total, dtype=jnp.int32)
    within = row_ids % (2 * freq_local)
    source = (group_index + group_size - row_ids // (2 * freq_local)) % group_size
    freq = source * freq_local + within // 2
    angles = jnp.arange(total, dtype=jnp.int32)
    phase = (angles[:, None] * freq[None, :] % total).astype(jnp.float32) * (2.0 * math.pi / total)
    cos_part = jnp.cos(phase).astype(jnp.bfloat16)
    sin_part = (-jnp.sin(phase)).astype(jnp.bfloat16)
    return jnp.where((within % 2 == 1)[None, :], sin_part, cos_part)


def iota(shape, dim):
    return lax.broadcasted_iota(jnp.int32, shape, dim)


def dot(a, b, dims):
    return lax.dot_general(a, b, (dims, ((), ())), precision=HIGHEST, preferred_element_type=jnp.float32)


def start_kernel(group_ref, coeffs_ref, vectors_ref, out_ref, same_ref, sq_ref):
    step = pl.program_id(0)

    @pl.when(step == 0)
    def _():
        sq_ref[...] = jnp.zeros_like(sq_ref)

    total = sq_ref[...]
    for k in range(coeffs_ref.shape[0]):
        values = coeffs_ref[k].astype(jnp.float32)
        total = total + values * values
    sq_ref[...] = total
    same_ref[...] = coeffs_ref[...]

    @pl.when(step == pl.num_programs(0) - 1)
    def _():
        block = sq_ref.shape[0]
        rows = vectors_ref.shape[0]
        total = dot(jnp.ones((8, sq_ref.shape[1]), jnp.float32), sq_ref[...], ((1,), (1,)))
        place = iota((rows, block), 1) == iota((rows, block), 0) + rows * group_ref[0]
        placed = dot(vectors_ref[...], place.astype(jnp.float32), ((0,), (0,)))
        for d in range(out_ref.shape[0]):
            out_ref[d, 0:8, :] = total
            out_ref[d, 8 : 8 + placed.shape[0], :] = placed


def start(group_index, coeffs, vectors, group_size):
    freq_local, block, channels = coeffs.shape
    rows = 8 + vectors.shape[1]
    steps = 5
    return pl.pallas_call(
        start_kernel,
        grid_spec=pltpu.PrefetchScalarGridSpec(
            num_scalar_prefetch=1,
            grid=(steps,),
            in_specs=[
                pl.BlockSpec((freq_local // steps, block, channels), lambda s, g: (s, 0, 0)),
                pl.BlockSpec(vectors.shape, lambda s, g: (0, 0)),
            ],
            out_specs=[
                pl.BlockSpec((group_size, rows, block), lambda s, g: (0, 0, 0)),
                pl.BlockSpec((freq_local // steps, block, channels), lambda s, g: (s, 0, 0)),
            ],
            scratch_shapes=[pltpu.VMEM((block, channels), jnp.float32)],
        ),
        out_shape=[pltpu.HBM((group_size, rows, block), jnp.float32), pltpu.HBM(coeffs.shape, coeffs.dtype)],
        compiler_params=pltpu.CompilerParams(vmem_limit_bytes=VMEM_LIMIT),
        name="start",
    )(group_index, coeffs, vectors)


def swapped(a):
    half = a.shape[1] // 2
    wide = a.astype(jnp.float32)
    turned = pltpu.roll(wide, half, 1)
    return jnp.where(iota(a.shape, 1) < half, turned, -turned).astype(a.dtype)


def upper_half(half, block):
    gap = (iota((half, block), 1) - iota((half, block), 0)) & (block - 1)
    return (gap >= 1) & (gap <= half)


def inverse_norm(total, count):
    block = total.shape[1]
    eye = iota((block, block), 0) == iota((block, block), 1)
    column = jnp.sum(jnp.where(eye, total, 0.0), axis=1, keepdims=True)
    return lax.rsqrt(column / count + epsilon)


def normalized(raw, inv_norm):
    return (raw.astype(jnp.float32) * inv_norm).astype(jnp.bfloat16)


def pair_terms(own, other):
    lhs = jnp.concatenate([own, swapped(own)], axis=0)
    pair = lax.dot_general(lhs, other, (((1,), (1,)), ((), ())), preferred_element_type=jnp.float32)
    return pair[: own.shape[0]], pair[own.shape[0] :]


def store_terms(out_ref, k, real, imag):
    parts = out_ref.shape[0]
    rows = real.shape[0] // parts
    for d in range(parts):
        both = jnp.concatenate([real[d * rows : (d + 1) * rows], imag[d * rows : (d + 1) * rows]], axis=0)
        out_ref[d, k * 2 * rows : (k + 1) * 2 * rows, :] = both.astype(jnp.bfloat16)


def cross_own_kernel(count, raw_ref, summed_ref, out_ref, unit_ref, inv_ref):
    block = raw_ref.shape[1]
    half = block // 2

    @pl.when(pl.program_id(0) == 0)
    def _():
        inv_ref[...] = jnp.broadcast_to(inverse_norm(summed_ref[0:1, :], count), inv_ref.shape)

    inv_norm = inv_ref[...]
    top = upper_half(half, block)
    for k in range(raw_ref.shape[0]):
        unit = normalized(raw_ref[k], inv_norm)
        unit_ref[k] = unit
        real, imag = pair_terms(unit, unit)
        store_terms(out_ref, k, jnp.where(top, real[:half], real[half:]), jnp.where(top, imag[:half], imag[half:]))


def cross_own(raw, summed, parts, steps):
    freq, block, channels = raw.shape
    rows = freq * block // parts
    spec = pl.BlockSpec((freq // steps, block, channels), lambda s: (s, 0, 0))
    return pl.pallas_call(
        functools.partial(cross_own_kernel, freq * parts * channels),
        grid=(steps,),
        in_specs=[spec, pl.BlockSpec(summed.shape, lambda s: (0, 0))],
        out_specs=[pl.BlockSpec((parts, rows // steps, block), lambda s: (0, s, 0)), spec],
        out_shape=[pltpu.HBM((parts, rows, block), jnp.bfloat16), pltpu.HBM(raw.shape, jnp.bfloat16)],
        scratch_shapes=[pltpu.VMEM((block, channels), jnp.float32)],
        compiler_params=pltpu.CompilerParams(vmem_limit_bytes=VMEM_LIMIT),
        name="cross_own",
    )(raw, summed)


def cross_next_kernel(count, group_ref, unit_ref, raw_ref, summed_ref, *refs):
    *out_refs, inv_ref, terms_ref = refs
    parts = len(out_refs)
    rows = raw_ref.shape[1] // parts

    @pl.when(pl.program_id(0) == 0)
    def _():
        inv_ref[...] = jnp.broadcast_to(inverse_norm(summed_ref[0:1, :], count), inv_ref.shape)

    inv_norm = inv_ref[...]
    at = [pl.multiple_of(rows * lax.rem(group_ref[0] + r, parts), rows) for r in range(parts)]
    for k in range(raw_ref.shape[0]):
        real, imag = pair_terms(unit_ref[k], normalized(raw_ref[k], inv_norm))
        terms_ref[k, 0] = real
        terms_ref[k, 1] = imag
    for k in range(raw_ref.shape[0]):
        for r in range(parts):
            for c in range(2):
                place = slice((2 * k + c) * rows, (2 * k + c + 1) * rows)
                out_refs[r][place, :] = terms_ref[k, c, pl.ds(at[r], rows), :].astype(jnp.bfloat16)


def cross_next(group_index, unit, raw, summed, parts, steps):
    freq, block, channels = raw.shape
    rows = freq * 2 * block // parts
    one = freq // steps
    spec = pl.BlockSpec((one, block, channels), lambda s, g: (s, 0, 0))
    return pl.pallas_call(
        functools.partial(cross_next_kernel, freq * parts * channels),
        grid_spec=pltpu.PrefetchScalarGridSpec(
            num_scalar_prefetch=1,
            grid=(steps,),
            in_specs=[spec, spec, pl.BlockSpec(summed.shape, lambda s, g: (0, 0))],
            out_specs=[pl.BlockSpec((rows // steps, block), lambda s, g: (s, 0))] * parts,
            scratch_shapes=[
                pltpu.VMEM((block, channels), jnp.float32),
                pltpu.VMEM((one, 2, block, block), jnp.float32),
            ],
        ),
        out_shape=[pltpu.HBM((rows, block), jnp.bfloat16)] * parts,
        compiler_params=pltpu.CompilerParams(vmem_limit_bytes=VMEM_LIMIT),
        name="cross_next",
    )(group_index, unit, raw, summed)


def affinities(load, pieces, piece_rows, trig_ref, held_ref, rows, width, factor):
    depth = trig_ref.shape[1]
    angles = trig_ref.shape[0]
    chunk = 16 * rows
    at = iota((chunk, chunk), 0)
    turn = (iota((chunk, chunk), 1) == (at & 15) * rows + (at >> 4)).astype(jnp.bfloat16)
    for c in range(depth // 16):
        begin, end = c * chunk, (c + 1) * chunk
        found = []
        for p in range(begin // piece_rows, (end - 1) // piece_rows + 1):
            low, high = max(begin, p * piece_rows), min(end, (p + 1) * piece_rows)
            found.append(load(p, low - p * piece_rows, high - low))
        piece = found[0] if len(found) == 1 else jnp.concatenate(found, axis=0)
        turned = jnp.dot(turn, piece, preferred_element_type=jnp.float32).astype(jnp.bfloat16)
        for i in range(rows):
            held_ref[c * 16 : (c + 1) * 16, i * width : (i + 1) * width] = turned[i * 16 : (i + 1) * 16]
    out = []
    for pair in range(rows // 2):
        corr = jnp.dot(
            trig_ref[...], held_ref[:, pair * 2 * width : (pair + 1) * 2 * width], preferred_element_type=jnp.float32
        )
        mean = jnp.sum(jnp.exp(factor * corr), axis=0, keepdims=True) * (1.0 / angles)
        out += [mean[:, :width], mean[:, width:]]
    return out


def own_kernel(factor, group_ref, terms_ref, trig_ref, out_ref, held_ref):
    parts, size, block = terms_ref.shape
    rows = out_ref.shape[0]
    sources = [lax.rem(group_ref[0] + (parts - p), parts) for p in range(parts)]

    def load(p, begin, count):
        return terms_ref[sources[p], begin : begin + count, :]

    means = affinities(load, parts, size, trig_ref, held_ref, rows, block, factor)
    for i in range(rows):
        out_ref[i : i + 1, :] = means[i]
    at = iota((rows, block), 0) + rows * group_ref[0]
    gap = (iota((rows, block), 1) - at) & (block - 1)
    out_ref[...] = jnp.where(gap == 0, 0.0, out_ref[...])


def own_part(group_index, terms, trig, factor):
    parts, _, block = terms.shape
    rows = block // 2 // parts
    return pl.pallas_call(
        functools.partial(own_kernel, factor),
        in_specs=[pl.BlockSpec(memory_space=pltpu.SMEM)] + [pl.BlockSpec(memory_space=pltpu.VMEM)] * 2,
        out_specs=pl.BlockSpec(memory_space=pltpu.VMEM),
        out_shape=jax.ShapeDtypeStruct((rows, block), jnp.float32),
        scratch_shapes=[pltpu.VMEM((trig.shape[1], rows * block), jnp.bfloat16)],
        compiler_params=pltpu.CompilerParams(vmem_limit_bytes=VMEM_LIMIT),
        name="own_part",
    )(group_index, terms, trig)


def next_kernel(factor, group_ref, trig_ref, own_ref, summed_ref, *refs):
    *piece_refs, out_ref, held_ref, wide_ref = refs
    rows = 16
    size, block = piece_refs[0].shape
    half = block // 2
    group = group_ref[0]

    def load(p, begin, count):
        return piece_refs[p][begin : begin + count, :]

    means = affinities(load, len(piece_refs), size, trig_ref, held_ref, rows, block, factor)
    for i in range(rows):
        out_ref[i : i + 1, :] = means[i]
    own = own_ref[...]
    at = iota((8, block), 0) + 8 * group
    gap = (iota((8, block), 1) - at) & (block - 1)
    top = (gap >= 1) & (gap <= half)
    upper, lower = jnp.where(top, own, 0.0), jnp.where(top, 0.0, own)
    wide_ref[...] = jnp.zeros_like(wide_ref)
    wide_ref[pl.ds(pl.multiple_of(rows * group, rows), rows), :] = out_ref[0:rows, :]
    own_at = pl.multiple_of(8 * group, 8)
    wide_ref[pl.ds(block + own_at, 8), :] = upper
    wide_ref[pl.ds(block + half + own_at, 8), :] = lower
    ones = jnp.ones((8, block), jnp.float32)
    by_row = dot(ones, wide_ref[...], ((1,), (1,)))
    degree = by_row[0:1, :block] + by_row[0:1, block:] + jnp.sum(own, axis=0, keepdims=True)
    out_ref[rows : rows + 8, :] = jnp.zeros((8, block), jnp.float32)
    out_ref[rows : rows + 1, :] = degree
    out_ref[rows + 1 : rows + 2, :] = jnp.sum(out_ref[0:rows, :], axis=0, keepdims=True)
    out_ref[rows + 8 :, :] = summed_ref[8:, :]


def next_part(group_index, pieces, trig, own, summed, factor):
    rows = 16
    block = pieces[0].shape[1]
    return pl.pallas_call(
        functools.partial(next_kernel, factor),
        in_specs=[pl.BlockSpec(memory_space=pltpu.SMEM)]
        + [pl.BlockSpec(memory_space=pltpu.VMEM)] * (3 + len(pieces)),
        out_specs=pl.BlockSpec(memory_space=pltpu.VMEM),
        out_shape=jax.ShapeDtypeStruct((rows + summed.shape[0], block), jnp.float32),
        scratch_shapes=[
            pltpu.VMEM((trig.shape[1], rows * block), jnp.bfloat16),
            pltpu.VMEM((2 * block, block), jnp.float32),
        ],
        compiler_params=pltpu.CompilerParams(vmem_limit_bytes=VMEM_LIMIT),
        name="next_part",
    )(group_index, trig, own, summed, *pieces)


def image_kernel(group_ref, parts_ref, before_ref, here_ref, after_ref, out_ref, own_ref, full_ref):
    groups, _, block = parts_ref.shape
    half = block // 2
    shares = parts_ref[0, 40:48, :]
    for s in range(groups):
        if s:
            shares = shares + parts_ref[s, 40:48, :]
        full_ref[0, 16 * s : 16 * s + 16, :] = parts_ref[s, 0:16, :]
        full_ref[1, 16 * s : 16 * s + 16, :] = parts_ref[s, 16:32, :]
        full_ref[2, 8 * s : 8 * s + 8, :] = parts_ref[s, 32:40, :]
    top = upper_half(half, block)
    own = full_ref[2, 0:half, :]
    full_ref[2, 0:half, :] = jnp.where(top, own, 0.0)
    full_ref[2, half:block, :] = jnp.where(top, 0.0, own)
    inv_root = lax.rsqrt(shares)
    scaled_before = before_ref[24:, :] * inv_root[0:1, :]
    scaled_own = here_ref[8:, :] * inv_root[1:2, :]
    scaled_after = after_ref[8:, :] * inv_root[2:3, :]
    along, across = ((1,), (1,)), ((1,), (0,))
    product = dot(scaled_own, full_ref[2], along) + dot(scaled_own, full_ref[2], across)
    product = product + dot(scaled_after, full_ref[0], along) + dot(scaled_before, full_ref[1], across)
    image = product * inv_root[1:2, :] * (3.0 * block)
    degree = shares[1:2, :]
    root_degree = jnp.sqrt(degree)
    degree_sum = jnp.sum(degree, axis=1, keepdims=True)
    proj = jnp.sum(root_degree * image, axis=1, keepdims=True)
    rest = image - root_degree * (proj / degree_sum)
    rest_sq = jnp.sum(rest * rest, axis=1, keepdims=True)
    count = image.shape[0]
    at, lane = iota((count, block), 0), iota((count, block), 1)
    stats = jnp.where(lane == at, proj, 0.0) + jnp.where(lane == at + count, rest_sq, 0.0)
    stats = jnp.sum(stats, axis=0, keepdims=True)
    stats = jnp.where(iota((1, block), 1) == 2 * count, degree_sum, stats)
    out_ref[...] = jnp.broadcast_to(stats, out_ref.shape)
    place = (lane == at + count * group_ref[0]).astype(jnp.float32)
    own_ref[0] = dot(place, image, along)
    own_ref[1] = dot(place, jnp.broadcast_to(root_degree, image.shape), along)


def image_part(group_index, parts, before, here, after, n_blk):
    groups, _, block = parts.shape
    count = here.shape[0] - 8
    return pl.pallas_call(
        image_kernel,
        in_specs=[pl.BlockSpec(memory_space=pltpu.SMEM)] + [pl.BlockSpec(memory_space=pltpu.VMEM)] * 4,
        out_specs=[pl.BlockSpec(memory_space=pltpu.VMEM)] * 2,
        out_shape=[
            jax.ShapeDtypeStruct((n_blk, block), jnp.float32),
            jax.ShapeDtypeStruct((2, count, count), jnp.float32),
        ],
        scratch_shapes=[pltpu.VMEM((3, block, block), jnp.float32)],
        compiler_params=pltpu.CompilerParams(vmem_limit_bytes=VMEM_LIMIT),
        name="image_part",
    )(group_index, parts, before, here, after)


def final_kernel(total_rows, stats_ref, own_ref, out_ref):
    count = out_ref.shape[1]
    stats = stats_ref[...]
    proj, rest_sq, degree = stats[:, :count], stats[:, count : 2 * count], stats[:, 2 * count : 2 * count + 1]
    ratio = jnp.sum(proj, axis=0, keepdims=True) / jnp.sum(degree, axis=0, keepdims=True)
    shift = proj / degree - ratio
    column_sq = jnp.sum(rest_sq + degree * (shift * shift), axis=0, keepdims=True)
    deflated = own_ref[0] - own_ref[1] * ratio
    out_ref[...] = deflated * lax.rsqrt(column_sq / total_rows + epsilon)


def final_part(stats, own, total_rows):
    count = own.shape[1]
    return pl.pallas_call(
        functools.partial(final_kernel, total_rows),
        in_specs=[pl.BlockSpec(memory_space=pltpu.VMEM)] * 2,
        out_specs=pl.BlockSpec(memory_space=pltpu.VMEM),
        out_shape=jax.ShapeDtypeStruct((count, count), jnp.float32),
        name="final_part",
    )(stats, own)


def per_device(coeffs, vectors):
    block, freq_local, channels = coeffs.shape
    group_size = lax.axis_size("grp")
    n_blk = lax.axis_size("blk")
    group_index = lax.axis_index("grp").astype(jnp.int32)[None]
    angles = freq_local * group_size
    factor = sharpness / math.sqrt(angles * channels)
    trig = trig_columns(freq_local, group_size, group_index[0])

    begun, by_freq = start(group_index, coeffs.transpose(1, 0, 2), vectors, group_size)
    summed = jnp.sum(lax.all_to_all(begun, "grp", 0, 0, tiled=True), axis=0)
    after_raw = passed_along(by_freq, "blk", -1)
    summed_after = passed_along(summed, "blk", -1)
    own_terms, own_unit = cross_own(by_freq, summed, group_size, 5)
    own_terms = lax.all_to_all(own_terms, "grp", 0, 0, tiled=True)
    next_terms = cross_next(group_index, own_unit, after_raw, summed_after, group_size, 5)
    next_terms = [next_terms[0]] + [passed_along(next_terms[r], "grp", r) for r in range(1, group_size)]
    own_aff = own_part(group_index, own_terms, trig, factor)
    found = next_part(group_index, next_terms, trig, own_aff, summed, factor)

    found_before = passed_along(found, "blk", 1)
    edge_after = passed_along(found[16:24], "blk", -1)
    edge_before = passed_along(found[16:24], "blk", 2)
    zeros = jnp.zeros((5, block), jnp.float32)
    shares = jnp.concatenate(
        [
            found_before[16:17] + edge_before[1:2],
            found[16:17] + found_before[17:18],
            edge_after[0:1] + found[17:18],
            zeros,
        ],
        axis=0,
    )
    sent = jnp.concatenate([found[:16], found_before[:16], own_aff, shares], axis=0)
    sent = jnp.broadcast_to(sent[None], (group_size,) + sent.shape)
    parts = lax.all_to_all(sent, "grp", 0, 0, tiled=True)
    stats, own = image_part(group_index, parts, found_before, summed, summed_after, n_blk)
    stats = lax.all_to_all(stats, "blk", 0, 0, tiled=True)
    return final_part(stats, own, block * n_blk)


def solution(mesh):
    placed = (P("blk", "grp", None), P(("blk", "grp"), None))
    return jax.shard_map(
        per_device, mesh=mesh, in_specs=placed, out_specs=P(("blk", "grp"), None), check_vma=False
    )
```

```python
import functools
import math

import jax
import jax.numpy as jnp
from jax import lax
from jax.experimental import pallas as pl
from jax.experimental.pallas import tpu as pltpu
from jax.sharding import PartitionSpec as P

sharpness = 2.5
epsilon = 1e-06
HIGHEST = lax.Precision.HIGHEST
VMEM_LIMIT = 24 * 1024 * 1024


def passed_along(block, axis, distance):
    devices = range(lax.axis_size(axis))
    route = [((i - distance) % len(devices), i) for i in devices]
    return lax.ppermute(block, axis, route)


def trig_columns(total):
    row_ids = jnp.arange(2 * total, dtype=jnp.int32)
    angles = jnp.arange(total, dtype=jnp.int32)
    phase = (angles[:, None] * (row_ids // 2)[None, :] % total).astype(jnp.float32) * (2.0 * math.pi / total)
    cos_part = jnp.cos(phase).astype(jnp.bfloat16)
    sin_part = (-jnp.sin(phase)).astype(jnp.bfloat16)
    return jnp.where((row_ids % 2 == 1)[None, :], sin_part, cos_part)


def iota(shape, dim):
    return lax.broadcasted_iota(jnp.int32, shape, dim)


def dot(a, b, dims):
    return lax.dot_general(a, b, (dims, ((), ())), precision=HIGHEST, preferred_element_type=jnp.float32)


def start_kernel(group_ref, squares_ref, vectors_ref, out_ref):
    block = squares_ref.shape[1]
    rows = vectors_ref.shape[0]
    total = jnp.broadcast_to(squares_ref[...], (8, block))
    place = iota((rows, block), 1) == iota((rows, block), 0) + rows * group_ref[0]
    placed = dot(vectors_ref[...], place.astype(jnp.float32), ((0,), (0,)))
    for d in range(out_ref.shape[0]):
        out_ref[d, 0:8, :] = total
        out_ref[d, 8 : 8 + placed.shape[0], :] = placed


def start(group_index, squares, vectors, group_size):
    shape = (group_size, 8 + vectors.shape[1], squares.shape[1])
    return pl.pallas_call(
        start_kernel,
        in_specs=[pl.BlockSpec(memory_space=pltpu.SMEM)] + [pl.BlockSpec(memory_space=pltpu.VMEM)] * 2,
        out_specs=pl.BlockSpec(memory_space=pltpu.VMEM),
        out_shape=jax.ShapeDtypeStruct(shape, jnp.float32),
        name="start",
    )(group_index, squares, vectors)


def swapped(a):
    half = a.shape[1] // 2
    wide = a.astype(jnp.float32)
    turned = pltpu.roll(wide, half, 1)
    return jnp.where(iota(a.shape, 1) < half, turned, -turned).astype(a.dtype)


def upper_half(half, block):
    gap = (iota((half, block), 1) - iota((half, block), 0)) & (block - 1)
    return (gap >= 1) & (gap <= half)


def pair_terms(own, other):
    lhs = jnp.concatenate([own, swapped(own)], axis=0)
    pair = lax.dot_general(lhs, other, (((1,), (1,)), ((), ())), preferred_element_type=jnp.float32)
    return pair[: own.shape[0]], pair[own.shape[0] :]


def store_terms(out_ref, k, real, imag):
    parts = out_ref.shape[0]
    rows = real.shape[0] // parts
    for d in range(parts):
        both = jnp.concatenate([real[d * rows : (d + 1) * rows], imag[d * rows : (d + 1) * rows]], axis=0)
        out_ref[d, k * 2 * rows : (k + 1) * 2 * rows, :] = both.astype(jnp.bfloat16)


def cross_kernel(folded, own_ref, other_ref, out_ref):
    block = own_ref.shape[1]
    half = block // 2
    for k in range(own_ref.shape[0]):
        real, imag = pair_terms(own_ref[k], other_ref[k])
        if folded:
            top = upper_half(half, block)
            real = jnp.where(top, real[:half], real[half:])
            imag = jnp.where(top, imag[:half], imag[half:])
        store_terms(out_ref, k, real, imag)


def cross(folded, own, other, parts, steps):
    freq, block, channels = own.shape
    rows = freq * (block if folded else 2 * block) // parts
    spec = pl.BlockSpec((freq // steps, block, channels), lambda s: (s, 0, 0))
    return pl.pallas_call(
        functools.partial(cross_kernel, folded),
        grid=(steps,),
        in_specs=[spec, spec],
        out_specs=pl.BlockSpec((parts, rows // steps, block), lambda s: (0, s, 0)),
        out_shape=pltpu.HBM((parts, rows, block), jnp.bfloat16),
        compiler_params=pltpu.CompilerParams(vmem_limit_bytes=VMEM_LIMIT),
        name="cross_own" if folded else "cross_next",
    )(own, other)


def affinities(load, pieces, piece_rows, trig_ref, held_ref, rows, width, factor):
    depth = trig_ref.shape[1]
    angles = trig_ref.shape[0]
    chunk = 16 * rows
    at = iota((chunk, chunk), 0)
    turn = (iota((chunk, chunk), 1) == (at & 15) * rows + (at >> 4)).astype(jnp.bfloat16)
    for c in range(depth // 16):
        begin, end = c * chunk, (c + 1) * chunk
        found = []
        for p in range(begin // piece_rows, (end - 1) // piece_rows + 1):
            low, high = max(begin, p * piece_rows), min(end, (p + 1) * piece_rows)
            found.append(load(p, low - p * piece_rows, high - low))
        piece = found[0] if len(found) == 1 else jnp.concatenate(found, axis=0)
        turned = jnp.dot(turn, piece, preferred_element_type=jnp.float32).astype(jnp.bfloat16)
        for i in range(rows):
            held_ref[c * 16 : (c + 1) * 16, i * width : (i + 1) * width] = turned[i * 16 : (i + 1) * 16]
    out = []
    for pair in range(rows // 2):
        corr = jnp.dot(
            trig_ref[...], held_ref[:, pair * 2 * width : (pair + 1) * 2 * width], preferred_element_type=jnp.float32
        )
        mean = jnp.sum(jnp.exp(factor * corr), axis=0, keepdims=True) * (1.0 / angles)
        out += [mean[:, :width], mean[:, width:]]
    return out


def own_kernel(factor, group_ref, terms_ref, trig_ref, out_ref, held_ref):
    parts, size, block = terms_ref.shape
    rows = out_ref.shape[0]

    def load(p, begin, count):
        return terms_ref[p, begin : begin + count, :]

    means = affinities(load, parts, size, trig_ref, held_ref, rows, block, factor)
    for i in range(rows):
        out_ref[i : i + 1, :] = means[i]
    at = iota((rows, block), 0) + rows * group_ref[0]
    gap = (iota((rows, block), 1) - at) & (block - 1)
    out_ref[...] = jnp.where(gap == 0, 0.0, out_ref[...])


def own_part(group_index, terms, trig, factor):
    parts, _, block = terms.shape
    rows = block // 2 // parts
    return pl.pallas_call(
        functools.partial(own_kernel, factor),
        in_specs=[pl.BlockSpec(memory_space=pltpu.SMEM)] + [pl.BlockSpec(memory_space=pltpu.VMEM)] * 2,
        out_specs=pl.BlockSpec(memory_space=pltpu.VMEM),
        out_shape=jax.ShapeDtypeStruct((rows, block), jnp.float32),
        scratch_shapes=[pltpu.VMEM((trig.shape[1], rows * block), jnp.bfloat16)],
        compiler_params=pltpu.CompilerParams(vmem_limit_bytes=VMEM_LIMIT),
        name="own_part",
    )(group_index, terms, trig)


def next_kernel(factor, group_ref, terms_ref, trig_ref, own_ref, summed_ref, out_ref, held_ref, wide_ref):
    rows = 16
    parts, size, block = terms_ref.shape
    half = block // 2
    group = group_ref[0]

    def load(p, begin, count):
        return terms_ref[p, begin : begin + count, :]

    means = affinities(load, parts, size, trig_ref, held_ref, rows, block, factor)
    for i in range(rows):
        out_ref[i : i + 1, :] = means[i]
    own = own_ref[...]
    at = iota((8, block), 0) + 8 * group
    gap = (iota((8, block), 1) - at) & (block - 1)
    top = (gap >= 1) & (gap <= half)
    upper, lower = jnp.where(top, own, 0.0), jnp.where(top, 0.0, own)
    wide_ref[...] = jnp.zeros_like(wide_ref)
    wide_ref[pl.ds(pl.multiple_of(rows * group, rows), rows), :] = out_ref[0:rows, :]
    own_at = pl.multiple_of(8 * group, 8)
    wide_ref[pl.ds(block + own_at, 8), :] = upper
    wide_ref[pl.ds(block + half + own_at, 8), :] = lower
    ones = jnp.ones((8, block), jnp.float32)
    by_row = dot(ones, wide_ref[...], ((1,), (1,)))
    degree = by_row[0:1, :block] + by_row[0:1, block:] + jnp.sum(own, axis=0, keepdims=True)
    out_ref[rows : rows + 8, :] = jnp.zeros((8, block), jnp.float32)
    out_ref[rows : rows + 1, :] = degree
    out_ref[rows + 1 : rows + 2, :] = jnp.sum(out_ref[0:rows, :], axis=0, keepdims=True)
    out_ref[rows + 8 :, :] = summed_ref[8:, :]


def next_part(group_index, terms, trig, own, summed, factor):
    rows = 16
    block = terms.shape[2]
    return pl.pallas_call(
        functools.partial(next_kernel, factor),
        in_specs=[pl.BlockSpec(memory_space=pltpu.SMEM)] + [pl.BlockSpec(memory_space=pltpu.VMEM)] * 4,
        out_specs=pl.BlockSpec(memory_space=pltpu.VMEM),
        out_shape=jax.ShapeDtypeStruct((rows + summed.shape[0], block), jnp.float32),
        scratch_shapes=[
            pltpu.VMEM((trig.shape[1], rows * block), jnp.bfloat16),
            pltpu.VMEM((2 * block, block), jnp.float32),
        ],
        compiler_params=pltpu.CompilerParams(vmem_limit_bytes=VMEM_LIMIT),
        name="next_part",
    )(group_index, terms, trig, own, summed)


def image_kernel(group_ref, parts_ref, before_ref, here_ref, after_ref, out_ref, own_ref, full_ref):
    groups, _, block = parts_ref.shape
    half = block // 2
    shares = parts_ref[0, 40:48, :]
    for s in range(groups):
        if s:
            shares = shares + parts_ref[s, 40:48, :]
        full_ref[0, 16 * s : 16 * s + 16, :] = parts_ref[s, 0:16, :]
        full_ref[1, 16 * s : 16 * s + 16, :] = parts_ref[s, 16:32, :]
        full_ref[2, 8 * s : 8 * s + 8, :] = parts_ref[s, 32:40, :]
    top = upper_half(half, block)
    own = full_ref[2, 0:half, :]
    full_ref[2, 0:half, :] = jnp.where(top, own, 0.0)
    full_ref[2, half:block, :] = jnp.where(top, 0.0, own)
    inv_root = lax.rsqrt(shares)
    scaled_before = before_ref[24:, :] * inv_root[0:1, :]
    scaled_own = here_ref[8:, :] * inv_root[1:2, :]
    scaled_after = after_ref[8:, :] * inv_root[2:3, :]
    along, across = ((1,), (1,)), ((1,), (0,))
    product = dot(scaled_own, full_ref[2], along) + dot(scaled_own, full_ref[2], across)
    product = product + dot(scaled_after, full_ref[0], along) + dot(scaled_before, full_ref[1], across)
    image = product * inv_root[1:2, :] * (3.0 * block)
    degree = shares[1:2, :]
    root_degree = jnp.sqrt(degree)
    degree_sum = jnp.sum(degree, axis=1, keepdims=True)
    proj = jnp.sum(root_degree * image, axis=1, keepdims=True)
    rest = image - root_degree * (proj / degree_sum)
    rest_sq = jnp.sum(rest * rest, axis=1, keepdims=True)
    count = image.shape[0]
    at, lane = iota((count, block), 0), iota((count, block), 1)
    stats = jnp.where(lane == at, proj, 0.0) + jnp.where(lane == at + count, rest_sq, 0.0)
    stats = jnp.sum(stats, axis=0, keepdims=True)
    stats = jnp.where(iota((1, block), 1) == 2 * count, degree_sum, stats)
    out_ref[...] = jnp.broadcast_to(stats, out_ref.shape)
    place = (lane == at + count * group_ref[0]).astype(jnp.float32)
    own_ref[0] = dot(place, image, along)
    own_ref[1] = dot(place, jnp.broadcast_to(root_degree, image.shape), along)


def image_part(group_index, parts, before, here, after, n_blk):
    groups, _, block = parts.shape
    count = here.shape[0] - 8
    return pl.pallas_call(
        image_kernel,
        in_specs=[pl.BlockSpec(memory_space=pltpu.SMEM)] + [pl.BlockSpec(memory_space=pltpu.VMEM)] * 4,
        out_specs=[pl.BlockSpec(memory_space=pltpu.VMEM)] * 2,
        out_shape=[
            jax.ShapeDtypeStruct((n_blk, block), jnp.float32),
            jax.ShapeDtypeStruct((2, count, count), jnp.float32),
        ],
        scratch_shapes=[pltpu.VMEM((3, block, block), jnp.float32)],
        compiler_params=pltpu.CompilerParams(vmem_limit_bytes=VMEM_LIMIT),
        name="image_part",
    )(group_index, parts, before, here, after)


def final_kernel(total_rows, stats_ref, own_ref, out_ref):
    count = out_ref.shape[1]
    stats = stats_ref[...]
    proj, rest_sq, degree = stats[:, :count], stats[:, count : 2 * count], stats[:, 2 * count : 2 * count + 1]
    ratio = jnp.sum(proj, axis=0, keepdims=True) / jnp.sum(degree, axis=0, keepdims=True)
    shift = proj / degree - ratio
    column_sq = jnp.sum(rest_sq + degree * (shift * shift), axis=0, keepdims=True)
    deflated = own_ref[0] - own_ref[1] * ratio
    out_ref[...] = deflated * lax.rsqrt(column_sq / total_rows + epsilon)


def final_part(stats, own, total_rows):
    count = own.shape[1]
    return pl.pallas_call(
        functools.partial(final_kernel, total_rows),
        in_specs=[pl.BlockSpec(memory_space=pltpu.VMEM)] * 2,
        out_specs=pl.BlockSpec(memory_space=pltpu.VMEM),
        out_shape=jax.ShapeDtypeStruct((count, count), jnp.float32),
        name="final_part",
    )(stats, own)


def per_device(coeffs, vectors):
    block, freq_local, channels = coeffs.shape
    group_size = lax.axis_size("grp")
    n_blk = lax.axis_size("blk")
    group_index = lax.axis_index("grp").astype(jnp.int32)[None]
    angles = freq_local * group_size
    factor = sharpness / math.sqrt(angles * channels)
    trig = trig_columns(angles)

    squares = jnp.einsum("ikc,ikc->i", coeffs, coeffs, preferred_element_type=jnp.float32)
    begun = start(group_index, squares[None], vectors, group_size)
    summed = jnp.sum(lax.all_to_all(begun, "grp", 0, 0, tiled=True), axis=0)
    inv_norm = lax.rsqrt(summed[0] / (angles * channels) + epsilon)
    own_unit = (coeffs.astype(jnp.float32) * inv_norm[:, None, None]).astype(jnp.bfloat16).transpose(1, 0, 2)
    after_unit = passed_along(own_unit, "blk", -1)
    own_terms = cross(True, own_unit, own_unit, group_size, 5)
    own_terms = lax.all_to_all(own_terms, "grp", 0, 0, tiled=True)
    next_terms = cross(False, own_unit, after_unit, group_size, 5)
    next_terms = lax.all_to_all(next_terms, "grp", 0, 0, tiled=True)
    own_aff = own_part(group_index, own_terms, trig, factor)
    found = next_part(group_index, next_terms, trig, own_aff, summed, factor)

    found_before = passed_along(found, "blk", 1)
    edge_after = passed_along(found[16:], "blk", -1)
    edge_before = passed_along(found[16:24], "blk", 2)
    zeros = jnp.zeros((5, block), jnp.float32)
    shares = jnp.concatenate(
        [
            found_before[16:17] + edge_before[1:2],
            found[16:17] + found_before[17:18],
            edge_after[0:1] + found[17:18],
            zeros,
        ],
        axis=0,
    )
    sent = jnp.concatenate([found[:16], found_before[:16], own_aff, shares], axis=0)
    sent = jnp.broadcast_to(sent[None], (group_size,) + sent.shape)
    parts = lax.all_to_all(sent, "grp", 0, 0, tiled=True)
    stats, own = image_part(group_index, parts, found_before, summed, edge_after, n_blk)
    stats = lax.all_to_all(stats, "blk", 0, 0, tiled=True)
    return final_part(stats, own, block * n_blk)


def solution(mesh):
    placed = (P("blk", "grp", None), P(("blk", "grp"), None))
    return jax.shard_map(
        per_device, mesh=mesh, in_specs=placed, out_specs=P(("blk", "grp"), None), check_vma=False
    )
```

```python
import functools
import math

import jax
import jax.numpy as jnp
from jax import lax
from jax.experimental import pallas as pl
from jax.experimental.pallas import tpu as pltpu
from jax.sharding import PartitionSpec as P

sharpness = 2.5
epsilon = 1e-06
HIGHEST = lax.Precision.HIGHEST
COST = pl.CostEstimate(flops=20000000000, transcendentals=0, bytes_accessed=6_000_000)
VMEM_LIMIT = 24 * 1024 * 1024


def passed_along(block, axis, distance):
    devices = range(lax.axis_size(axis))
    route = [((i - distance) % len(devices), i) for i in devices]
    return lax.ppermute(block, axis, route)


def trig_columns(freq_local, group_size, group_index):
    total = freq_local * group_size
    half_width = (total + 127) // 128 * 128
    column = jnp.arange(2 * half_width, dtype=jnp.int32)
    place = column // half_width * total + column % half_width
    within = place % (2 * freq_local)
    source = (group_index + group_size - place // (2 * freq_local) % group_size) % group_size
    freq = source * freq_local + within // 2
    angles = jnp.arange(total, dtype=jnp.int32)
    phase = (angles[:, None] * freq[None, :] % total).astype(jnp.float32) * (2.0 * math.pi / total)
    cos_part = jnp.cos(phase).astype(jnp.bfloat16)
    sin_part = (-jnp.sin(phase)).astype(jnp.bfloat16)
    found = jnp.where((within % 2 == 1)[None, :], sin_part, cos_part)
    return jnp.where((column % half_width < total)[None, :], found, jnp.zeros_like(found))


def iota(shape, dim):
    return lax.broadcasted_iota(jnp.int32, shape, dim)


def dot(a, b, dims):
    return lax.dot_general(a, b, (dims, ((), ())), precision=HIGHEST, preferred_element_type=jnp.float32)


def start_kernel(group_ref, coeffs_ref, vectors_ref, out_ref, same_ref, sq_ref):
    step = pl.program_id(0)

    @pl.when(step == 0)
    def _():
        sq_ref[...] = jnp.zeros_like(sq_ref)

    total = sq_ref[...]
    for k in range(coeffs_ref.shape[0]):
        values = coeffs_ref[k].astype(jnp.float32)
        total = total + values * values
    sq_ref[...] = total
    same_ref[...] = coeffs_ref[...]

    @pl.when(step == pl.num_programs(0) - 1)
    def _():
        block = sq_ref.shape[0]
        rows = vectors_ref.shape[0]
        total = dot(jnp.ones((8, sq_ref.shape[1]), jnp.float32), sq_ref[...], ((1,), (1,)))
        place = iota((rows, block), 1) == iota((rows, block), 0) + rows * group_ref[0]
        placed = dot(vectors_ref[...], place.astype(jnp.float32), ((0,), (0,)))
        for d in range(out_ref.shape[0]):
            out_ref[d, 0:8, :] = total
            out_ref[d, 8 : 8 + placed.shape[0], :] = placed


def start(group_index, coeffs, vectors, group_size):
    freq_local, block, channels = coeffs.shape
    rows = 8 + vectors.shape[1]
    steps = 5
    return pl.pallas_call(
        start_kernel,
        grid_spec=pltpu.PrefetchScalarGridSpec(
            num_scalar_prefetch=1,
            grid=(steps,),
            in_specs=[
                pl.BlockSpec((freq_local // steps, block, channels), lambda s, g: (s, 0, 0)),
                pl.BlockSpec(vectors.shape, lambda s, g: (0, 0)),
            ],
            out_specs=[
                pl.BlockSpec((group_size, rows, block), lambda s, g: (0, 0, 0)),
                pl.BlockSpec((freq_local // steps, block, channels), lambda s, g: (s, 0, 0)),
            ],
            scratch_shapes=[pltpu.VMEM((block, channels), jnp.float32)],
        ),
        out_shape=[pltpu.HBM((group_size, rows, block), jnp.float32), pltpu.HBM(coeffs.shape, coeffs.dtype)],
        compiler_params=pltpu.CompilerParams(vmem_limit_bytes=VMEM_LIMIT),
        name="start",
    )(group_index, coeffs, vectors)


def swapped(a):
    half = a.shape[1] // 2
    wide = a.astype(jnp.float32)
    turned = pltpu.roll(wide, half, 1)
    return jnp.where(iota(a.shape, 1) < half, turned, -turned).astype(a.dtype)


def upper_half(half, block):
    gap = (iota((half, block), 1) - iota((half, block), 0)) & (block - 1)
    return (gap >= 1) & (gap <= half)


def inverse_norm(total, count):
    block = total.shape[1]
    eye = iota((block, block), 0) == iota((block, block), 1)
    column = jnp.sum(jnp.where(eye, total, 0.0), axis=1, keepdims=True)
    return lax.rsqrt(column / count + epsilon)


def normalized(raw, inv_norm):
    return (raw.astype(jnp.float32) * inv_norm).astype(jnp.bfloat16)


def pair_terms(own, other):
    lhs = jnp.concatenate([own, swapped(own)], axis=0)
    pair = lax.dot_general(lhs, other, (((1,), (1,)), ((), ())), preferred_element_type=jnp.float32)
    return pair[: own.shape[0]], pair[own.shape[0] :]


def store_terms(out_ref, k, real, imag):
    parts = out_ref.shape[0]
    rows = real.shape[0] // parts
    for d in range(parts):
        both = jnp.concatenate([real[d * rows : (d + 1) * rows], imag[d * rows : (d + 1) * rows]], axis=0)
        out_ref[d, k * 2 * rows : (k + 1) * 2 * rows, :] = both.astype(jnp.bfloat16)


def cross_own_kernel(count, raw_ref, summed_ref, out_ref, unit_ref, inv_ref):
    block = raw_ref.shape[1]
    half = block // 2

    @pl.when(pl.program_id(0) == 0)
    def _():
        inv_ref[...] = jnp.broadcast_to(inverse_norm(summed_ref[0:1, :], count), inv_ref.shape)

    inv_norm = inv_ref[...]
    top = upper_half(half, block)
    for k in range(raw_ref.shape[0]):
        unit = normalized(raw_ref[k], inv_norm)
        unit_ref[k] = unit
        real, imag = pair_terms(unit, unit)
        store_terms(out_ref, k, jnp.where(top, real[:half], real[half:]), jnp.where(top, imag[:half], imag[half:]))


def cross_own(raw, summed, parts, steps):
    freq, block, channels = raw.shape
    rows = freq * block // parts
    spec = pl.BlockSpec((freq // steps, block, channels), lambda s: (s, 0, 0))
    return pl.pallas_call(
        functools.partial(cross_own_kernel, freq * parts * channels),
        grid=(steps,),
        in_specs=[spec, pl.BlockSpec(summed.shape, lambda s: (0, 0))],
        out_specs=[pl.BlockSpec((parts, rows // steps, block), lambda s: (0, s, 0)), spec],
        out_shape=[pltpu.HBM((parts, rows, block), jnp.bfloat16), pltpu.HBM(raw.shape, jnp.bfloat16)],
        scratch_shapes=[pltpu.VMEM((block, channels), jnp.float32)],
        compiler_params=pltpu.CompilerParams(vmem_limit_bytes=VMEM_LIMIT),
        cost_estimate=COST,
        name="cross_own",
    )(raw, summed)


def cross_next_kernel(count, group_ref, unit_ref, raw_ref, summed_ref, *refs):
    *out_refs, inv_ref, terms_ref = refs
    parts = len(out_refs)
    rows = raw_ref.shape[1] // parts

    @pl.when(pl.program_id(0) == 0)
    def _():
        inv_ref[...] = jnp.broadcast_to(inverse_norm(summed_ref[0:1, :], count), inv_ref.shape)

    inv_norm = inv_ref[...]
    at = [pl.multiple_of(rows * lax.rem(group_ref[0] + r, parts), rows) for r in range(parts)]
    for k in range(raw_ref.shape[0]):
        real, imag = pair_terms(unit_ref[k], normalized(raw_ref[k], inv_norm))
        terms_ref[k, 0] = real
        terms_ref[k, 1] = imag
    for k in range(raw_ref.shape[0]):
        for r in range(parts):
            for c in range(2):
                place = slice((2 * k + c) * rows, (2 * k + c + 1) * rows)
                out_refs[r][place, :] = terms_ref[k, c, pl.ds(at[r], rows), :].astype(jnp.bfloat16)


def cross_next(group_index, unit, raw, summed, parts, steps):
    freq, block, channels = raw.shape
    rows = freq * 2 * block // parts
    one = freq // steps
    spec = pl.BlockSpec((one, block, channels), lambda s, g: (s, 0, 0))
    return pl.pallas_call(
        functools.partial(cross_next_kernel, freq * parts * channels),
        grid_spec=pltpu.PrefetchScalarGridSpec(
            num_scalar_prefetch=1,
            grid=(steps,),
            in_specs=[spec, spec, pl.BlockSpec(summed.shape, lambda s, g: (0, 0))],
            out_specs=[pl.BlockSpec((rows // steps, block), lambda s, g: (s, 0))] * parts,
            scratch_shapes=[
                pltpu.VMEM((block, channels), jnp.float32),
                pltpu.VMEM((one, 2, block, block), jnp.float32),
            ],
        ),
        out_shape=[pltpu.HBM((rows, block), jnp.bfloat16)] * parts,
        compiler_params=pltpu.CompilerParams(vmem_limit_bytes=VMEM_LIMIT),
        cost_estimate=COST,
        name="cross_next",
    )(group_index, unit, raw, summed)


def turn(load, pieces, piece_rows, held_ref, base, width, rows, block):
    chunk = 16 * rows
    at = iota((chunk, chunk), 0)
    matrix = (iota((chunk, chunk), 1) == (at & 15) * rows + (at >> 4)).astype(jnp.bfloat16)
    total = pieces * piece_rows
    for c in range(-(-total // chunk)):
        begin, end = c * chunk, min((c + 1) * chunk, total)
        found = []
        for p in range(begin // piece_rows, (end - 1) // piece_rows + 1):
            low, high = max(begin, p * piece_rows), min(end, (p + 1) * piece_rows)
            found.append(load(p, low - p * piece_rows, high - low))
        piece = found[0] if len(found) == 1 else jnp.concatenate(found, axis=0)
        turned = jnp.dot(matrix[:, : end - begin], piece, preferred_element_type=jnp.float32).astype(jnp.bfloat16)
        for i in range(rows):
            held_ref[base + c * 16 : base + (c + 1) * 16, i * block : (i + 1) * block] = turned[i * 16 : (i + 1) * 16]
    used = -(-total // chunk) * 16
    if used < width:
        held_ref[base + used : base + width, :] = jnp.zeros((width - used, rows * block), jnp.bfloat16)


def mean_exp(corr, factor):
    return jnp.sum(jnp.exp(factor * corr), axis=0, keepdims=True) * (1.0 / corr.shape[0])


def own_kernel(factor, group_ref, terms_ref, trig_ref, out_ref, held_ref):
    parts, size, block = terms_ref.shape
    rows = out_ref.shape[0]
    sources = [lax.rem(group_ref[0] + (parts - p), parts) for p in range(parts)]

    def load(p, begin, count):
        return terms_ref[sources[p], begin : begin + count, :]

    half = parts // 2
    width = trig_ref.shape[1] // 2
    for h in range(2):
        turn(lambda p, *where: load(h * half + p, *where), half, size, held_ref, h * width, width, rows, block)
    for i in range(0, rows, 2):
        corr = jnp.dot(trig_ref[...], held_ref[:, i * block : (i + 2) * block], preferred_element_type=jnp.float32)
        mean = mean_exp(corr, factor)
        out_ref[i : i + 1, :] = mean[:, :block]
        out_ref[i + 1 : i + 2, :] = mean[:, block:]
    at = iota((rows, block), 0) + rows * group_ref[0]
    gap = (iota((rows, block), 1) - at) & (block - 1)
    out_ref[...] = jnp.where(gap == 0, 0.0, out_ref[...])


def own_part(group_index, terms, trig, factor):
    parts, _, block = terms.shape
    rows = block // 2 // parts
    return pl.pallas_call(
        functools.partial(own_kernel, factor),
        in_specs=[pl.BlockSpec(memory_space=pltpu.SMEM)] + [pl.BlockSpec(memory_space=pltpu.VMEM)] * 2,
        out_specs=pl.BlockSpec(memory_space=pltpu.VMEM),
        out_shape=jax.ShapeDtypeStruct((rows, block), jnp.float32),
        scratch_shapes=[pltpu.VMEM((trig.shape[1], rows * block), jnp.bfloat16)],
        compiler_params=pltpu.CompilerParams(vmem_limit_bytes=VMEM_LIMIT),
        name="own_part",
    )(group_index, terms, trig)


def first_kernel(trig_ref, *refs):
    *piece_refs, out_ref, held_ref = refs
    rows = 16
    size, block = piece_refs[0].shape
    width = held_ref.shape[0]
    turn(lambda p, b, n: piece_refs[p][b : b + n, :], len(piece_refs), size, held_ref, 0, width, rows, block)
    for i in range(0, rows, 2):
        cut = slice(i * block, (i + 2) * block)
        out_ref[:, cut] = jnp.dot(trig_ref[:, :width], held_ref[:, cut], preferred_element_type=jnp.float32)


def first_part(pieces, trig):
    rows = 16
    block = pieces[0].shape[1]
    return pl.pallas_call(
        first_kernel,
        in_specs=[pl.BlockSpec(memory_space=pltpu.VMEM)] * (1 + len(pieces)),
        out_specs=pl.BlockSpec(memory_space=pltpu.VMEM),
        out_shape=jax.ShapeDtypeStruct((trig.shape[0], rows * block), jnp.float32),
        scratch_shapes=[pltpu.VMEM((trig.shape[1] // 2, rows * block), jnp.bfloat16)],
        compiler_params=pltpu.CompilerParams(vmem_limit_bytes=VMEM_LIMIT),
        name="first_part",
    )(trig, *pieces)


def next_kernel(factor, group_ref, trig_ref, own_ref, summed_ref, share_ref, *refs):
    *piece_refs, out_ref, held_ref, wide_ref = refs
    rows = 16
    size, block = piece_refs[0].shape
    half = block // 2
    group = group_ref[0]
    width = held_ref.shape[0]
    turn(lambda p, b, n: piece_refs[p][b : b + n, :], len(piece_refs), size, held_ref, 0, width, rows, block)
    for i in range(0, rows, 2):
        cut = slice(i * block, (i + 2) * block)
        corr = jnp.dot(trig_ref[:, width:], held_ref[:, cut], preferred_element_type=jnp.float32)
        mean = mean_exp(share_ref[:, cut] + corr, factor)
        out_ref[i : i + 1, :] = mean[:, :block]
        out_ref[i + 1 : i + 2, :] = mean[:, block:]
    own = own_ref[...]
    at = iota((8, block), 0) + 8 * group
    gap = (iota((8, block), 1) - at) & (block - 1)
    top = (gap >= 1) & (gap <= half)
    upper, lower = jnp.where(top, own, 0.0), jnp.where(top, 0.0, own)
    wide_ref[...] = jnp.zeros_like(wide_ref)
    wide_ref[pl.ds(pl.multiple_of(rows * group, rows), rows), :] = out_ref[0:rows, :]
    own_at = pl.multiple_of(8 * group, 8)
    wide_ref[pl.ds(block + own_at, 8), :] = upper
    wide_ref[pl.ds(block + half + own_at, 8), :] = lower
    ones = jnp.ones((8, block), jnp.float32)
    by_row = dot(ones, wide_ref[...], ((1,), (1,)))
    degree = by_row[0:1, :block] + by_row[0:1, block:] + jnp.sum(own, axis=0, keepdims=True)
    out_ref[rows : rows + 8, :] = jnp.zeros((8, block), jnp.float32)
    out_ref[rows : rows + 1, :] = degree
    out_ref[rows + 1 : rows + 2, :] = jnp.sum(out_ref[0:rows, :], axis=0, keepdims=True)
    out_ref[rows + 8 :, :] = summed_ref[8:, :]


def next_part(group_index, share, pieces, trig, own, summed, factor):
    rows = 16
    block = pieces[0].shape[1]
    return pl.pallas_call(
        functools.partial(next_kernel, factor),
        in_specs=[pl.BlockSpec(memory_space=pltpu.SMEM)]
        + [pl.BlockSpec(memory_space=pltpu.VMEM)] * (4 + len(pieces)),
        out_specs=pl.BlockSpec(memory_space=pltpu.VMEM),
        out_shape=jax.ShapeDtypeStruct((rows + summed.shape[0], block), jnp.float32),
        scratch_shapes=[
            pltpu.VMEM((trig.shape[1] // 2, rows * block), jnp.bfloat16),
            pltpu.VMEM((2 * block, block), jnp.float32),
        ],
        compiler_params=pltpu.CompilerParams(vmem_limit_bytes=VMEM_LIMIT),
        name="next_part",
    )(group_index, trig, own, summed, share, *pieces)


def image_kernel(group_ref, parts_ref, before_ref, here_ref, after_ref, out_ref, own_ref, full_ref):
    groups, _, block = parts_ref.shape
    half = block // 2
    shares = parts_ref[0, 40:48, :]
    for s in range(groups):
        if s:
            shares = shares + parts_ref[s, 40:48, :]
        full_ref[0, 16 * s : 16 * s + 16, :] = parts_ref[s, 0:16, :]
        full_ref[1, 16 * s : 16 * s + 16, :] = parts_ref[s, 16:32, :]
        full_ref[2, 8 * s : 8 * s + 8, :] = parts_ref[s, 32:40, :]
    top = upper_half(half, block)
    own = full_ref[2, 0:half, :]
    full_ref[2, 0:half, :] = jnp.where(top, own, 0.0)
    full_ref[2, half:block, :] = jnp.where(top, 0.0, own)
    inv_root = lax.rsqrt(shares)
    scaled_before = before_ref[24:, :] * inv_root[0:1, :]
    scaled_own = here_ref[8:, :] * inv_root[1:2, :]
    scaled_after = after_ref[8:, :] * inv_root[2:3, :]
    along, across = ((1,), (1,)), ((1,), (0,))
    product = dot(scaled_own, full_ref[2], along) + dot(scaled_own, full_ref[2], across)
    product = product + dot(scaled_after, full_ref[0], along) + dot(scaled_before, full_ref[1], across)
    image = product * inv_root[1:2, :] * (3.0 * block)
    degree = shares[1:2, :]
    root_degree = jnp.sqrt(degree)
    degree_sum = jnp.sum(degree, axis=1, keepdims=True)
    proj = jnp.sum(root_degree * image, axis=1, keepdims=True)
    rest = image - root_degree * (proj / degree_sum)
    rest_sq = jnp.sum(rest * rest, axis=1, keepdims=True)
    count = image.shape[0]
    at, lane = iota((count, block), 0), iota((count, block), 1)
    stats = jnp.where(lane == at, proj, 0.0) + jnp.where(lane == at + count, rest_sq, 0.0)
    stats = jnp.sum(stats, axis=0, keepdims=True)
    stats = jnp.where(iota((1, block), 1) == 2 * count, degree_sum, stats)
    out_ref[...] = jnp.broadcast_to(stats, out_ref.shape)
    place = (lane == at + count * group_ref[0]).astype(jnp.float32)
    own_ref[0] = dot(place, image, along)
    own_ref[1] = dot(place, jnp.broadcast_to(root_degree, image.shape), along)


def image_part(group_index, parts, before, here, after, n_blk):
    groups, _, block = parts.shape
    count = here.shape[0] - 8
    return pl.pallas_call(
        image_kernel,
        in_specs=[pl.BlockSpec(memory_space=pltpu.SMEM)] + [pl.BlockSpec(memory_space=pltpu.VMEM)] * 4,
        out_specs=[pl.BlockSpec(memory_space=pltpu.VMEM)] * 2,
        out_shape=[
            jax.ShapeDtypeStruct((n_blk, block), jnp.float32),
            jax.ShapeDtypeStruct((2, count, count), jnp.float32),
        ],
        scratch_shapes=[pltpu.VMEM((3, block, block), jnp.float32)],
        compiler_params=pltpu.CompilerParams(vmem_limit_bytes=VMEM_LIMIT),
        name="image_part",
    )(group_index, parts, before, here, after)


def final_kernel(total_rows, stats_ref, own_ref, out_ref):
    count = out_ref.shape[1]
    stats = stats_ref[...]
    proj, rest_sq, degree = stats[:, :count], stats[:, count : 2 * count], stats[:, 2 * count : 2 * count + 1]
    ratio = jnp.sum(proj, axis=0, keepdims=True) / jnp.sum(degree, axis=0, keepdims=True)
    shift = proj / degree - ratio
    column_sq = jnp.sum(rest_sq + degree * (shift * shift), axis=0, keepdims=True)
    deflated = own_ref[0] - own_ref[1] * ratio
    out_ref[...] = deflated * lax.rsqrt(column_sq / total_rows + epsilon)


def final_part(stats, own, total_rows):
    count = own.shape[1]
    return pl.pallas_call(
        functools.partial(final_kernel, total_rows),
        in_specs=[pl.BlockSpec(memory_space=pltpu.VMEM)] * 2,
        out_specs=pl.BlockSpec(memory_space=pltpu.VMEM),
        out_shape=jax.ShapeDtypeStruct((count, count), jnp.float32),
        name="final_part",
    )(stats, own)


def per_device(coeffs, vectors):
    block, freq_local, channels = coeffs.shape
    group_size = lax.axis_size("grp")
    n_blk = lax.axis_size("blk")
    group_index = lax.axis_index("grp").astype(jnp.int32)[None]
    angles = freq_local * group_size
    factor = sharpness / math.sqrt(angles * channels)
    trig = trig_columns(freq_local, group_size, group_index[0])

    begun, by_freq = start(group_index, coeffs.transpose(1, 0, 2), vectors, group_size)
    summed = jnp.sum(lax.all_to_all(begun, "grp", 0, 0, tiled=True), axis=0)
    after_raw = passed_along(by_freq, "blk", -1)
    summed_after = passed_along(summed, "blk", -1)
    own_terms, own_unit = cross_own(by_freq, summed, group_size, 5)
    own_terms = lax.all_to_all(own_terms, "grp", 0, 0, tiled=True)
    next_terms = cross_next(group_index, own_unit, after_raw, summed_after, group_size, 5)
    next_terms = [next_terms[0]] + [passed_along(next_terms[r], "grp", r) for r in range(1, group_size)]
    own_aff = own_part(group_index, own_terms, trig, factor)
    share = first_part(next_terms[: group_size // 2], trig)
    found = next_part(group_index, share, next_terms[group_size // 2 :], trig, own_aff, summed, factor)

    found_before = passed_along(found, "blk", 1)
    edge_after = passed_along(found[16:24], "blk", -1)
    edge_before = passed_along(found[16:24], "blk", 2)
    zeros = jnp.zeros((5, block), jnp.float32)
    shares = jnp.concatenate(
        [
            found_before[16:17] + edge_before[1:2],
            found[16:17] + found_before[17:18],
            edge_after[0:1] + found[17:18],
            zeros,
        ],
        axis=0,
    )
    sent = jnp.concatenate([found[:16], found_before[:16], own_aff, shares], axis=0)
    sent = jnp.broadcast_to(sent[None], (group_size,) + sent.shape)
    parts = lax.all_to_all(sent, "grp", 0, 0, tiled=True)
    stats, own = image_part(group_index, parts, found_before, summed, summed_after, n_blk)
    stats = lax.all_to_all(stats, "blk", 0, 0, tiled=True)
    return final_part(stats, own, block * n_blk)


def solution(mesh):
    placed = (P("blk", "grp", None), P(("blk", "grp"), None))
    return jax.shard_map(
        per_device, mesh=mesh, in_specs=placed, out_specs=P(("blk", "grp"), None), check_vma=False
    )
```

```python
import functools
import math

import jax
import jax.numpy as jnp
from jax import lax
from jax.experimental import pallas as pl
from jax.experimental.pallas import tpu as pltpu
from jax.sharding import PartitionSpec as P

sharpness = 2.5
epsilon = 1e-06
HIGHEST = lax.Precision.HIGHEST
COST = pl.CostEstimate(flops=20000000000, transcendentals=0, bytes_accessed=6_000_000)
VMEM_LIMIT = 24 * 1024 * 1024


def passed_along(block, axis, distance):
    devices = range(lax.axis_size(axis))
    route = [((i - distance) % len(devices), i) for i in devices]
    return lax.ppermute(block, axis, route)


def trig_columns(freq_local, group_size, group_index):
    total = freq_local * group_size
    half_width = (total + 127) // 128 * 128
    column = jnp.arange(2 * half_width, dtype=jnp.int32)
    place = column // half_width * total + column % half_width
    within = place % (2 * freq_local)
    source = (group_index + group_size - place // (2 * freq_local) % group_size) % group_size
    freq = source * freq_local + within // 2
    angles = jnp.arange(total, dtype=jnp.int32)
    phase = (angles[:, None] * freq[None, :] % total).astype(jnp.float32) * (2.0 * math.pi / total)
    cos_part = jnp.cos(phase).astype(jnp.bfloat16)
    sin_part = (-jnp.sin(phase)).astype(jnp.bfloat16)
    found = jnp.where((within % 2 == 1)[None, :], sin_part, cos_part)
    return jnp.where((column % half_width < total)[None, :], found, jnp.zeros_like(found))


def iota(shape, dim):
    return lax.broadcasted_iota(jnp.int32, shape, dim)


def dot(a, b, dims):
    return lax.dot_general(a, b, (dims, ((), ())), precision=HIGHEST, preferred_element_type=jnp.float32)


def start_kernel(group_ref, coeffs_ref, vectors_ref, out_ref, same_ref, sq_ref):
    step = pl.program_id(0)

    @pl.when(step == 0)
    def _():
        sq_ref[...] = jnp.zeros_like(sq_ref)

    total = sq_ref[...]
    for k in range(coeffs_ref.shape[0]):
        values = coeffs_ref[k].astype(jnp.float32)
        total = total + values * values
    sq_ref[...] = total
    same_ref[...] = coeffs_ref[...]

    @pl.when(step == pl.num_programs(0) - 1)
    def _():
        block = sq_ref.shape[0]
        rows = vectors_ref.shape[0]
        total = dot(jnp.ones((8, sq_ref.shape[1]), jnp.float32), sq_ref[...], ((1,), (1,)))
        place = iota((rows, block), 1) == iota((rows, block), 0) + rows * group_ref[0]
        placed = dot(vectors_ref[...], place.astype(jnp.float32), ((0,), (0,)))
        for d in range(out_ref.shape[0]):
            out_ref[d, 0:8, :] = total
            out_ref[d, 8 : 8 + placed.shape[0], :] = placed


def start(group_index, coeffs, vectors, group_size):
    freq_local, block, channels = coeffs.shape
    rows = 8 + vectors.shape[1]
    steps = 3
    return pl.pallas_call(
        start_kernel,
        grid_spec=pltpu.PrefetchScalarGridSpec(
            num_scalar_prefetch=1,
            grid=(steps,),
            in_specs=[
                pl.BlockSpec((freq_local // steps, block, channels), lambda s, g: (s, 0, 0)),
                pl.BlockSpec(vectors.shape, lambda s, g: (0, 0)),
            ],
            out_specs=[
                pl.BlockSpec((group_size, rows, block), lambda s, g: (0, 0, 0)),
                pl.BlockSpec((freq_local // steps, block, channels), lambda s, g: (s, 0, 0)),
            ],
            scratch_shapes=[pltpu.VMEM((block, channels), jnp.float32)],
        ),
        out_shape=[pltpu.HBM((group_size, rows, block), jnp.float32), pltpu.HBM(coeffs.shape, coeffs.dtype)],
        compiler_params=pltpu.CompilerParams(vmem_limit_bytes=VMEM_LIMIT),
        name="start",
    )(group_index, coeffs, vectors)


def swapped(a):
    half = a.shape[1] // 2
    wide = a.astype(jnp.float32)
    turned = pltpu.roll(wide, half, 1)
    return jnp.where(iota(a.shape, 1) < half, turned, -turned).astype(a.dtype)


def upper_half(half, block):
    gap = (iota((half, block), 1) - iota((half, block), 0)) & (block - 1)
    return (gap >= 1) & (gap <= half)


def inverse_norm(total, count):
    block = total.shape[1]
    eye = iota((block, block), 0) == iota((block, block), 1)
    column = jnp.sum(jnp.where(eye, total, 0.0), axis=1, keepdims=True)
    return lax.rsqrt(column / count + epsilon)


def normalized(raw, inv_norm):
    return (raw.astype(jnp.float32) * inv_norm).astype(jnp.bfloat16)


def pair_terms(own, other):
    lhs = jnp.concatenate([own, swapped(own)], axis=0)
    pair = lax.dot_general(lhs, other, (((1,), (1,)), ((), ())), preferred_element_type=jnp.float32)
    return pair[: own.shape[0]], pair[own.shape[0] :]


def store_terms(out_ref, k, real, imag):
    parts = out_ref.shape[0]
    rows = real.shape[0] // parts
    for d in range(parts):
        both = jnp.concatenate([real[d * rows : (d + 1) * rows], imag[d * rows : (d + 1) * rows]], axis=0)
        out_ref[d, k * 2 * rows : (k + 1) * 2 * rows, :] = both.astype(jnp.bfloat16)


def cross_own_kernel(count, raw_ref, summed_ref, out_ref, unit_ref, inv_ref):
    block = raw_ref.shape[1]
    half = block // 2

    @pl.when(pl.program_id(0) == 0)
    def _():
        inv_ref[...] = jnp.broadcast_to(inverse_norm(summed_ref[0:1, :], count), inv_ref.shape)

    inv_norm = inv_ref[...]
    top = upper_half(half, block)
    for k in range(raw_ref.shape[0]):
        unit = normalized(raw_ref[k], inv_norm)
        unit_ref[k] = unit
        real, imag = pair_terms(unit, unit)
        store_terms(out_ref, k, jnp.where(top, real[:half], real[half:]), jnp.where(top, imag[:half], imag[half:]))


def cross_own(raw, summed, parts, steps):
    freq, block, channels = raw.shape
    rows = freq * block // parts
    spec = pl.BlockSpec((freq // steps, block, channels), lambda s: (s, 0, 0))
    return pl.pallas_call(
        functools.partial(cross_own_kernel, freq * parts * channels),
        grid=(steps,),
        in_specs=[spec, pl.BlockSpec(summed.shape, lambda s: (0, 0))],
        out_specs=[pl.BlockSpec((parts, rows // steps, block), lambda s: (0, s, 0)), spec],
        out_shape=[pltpu.HBM((parts, rows, block), jnp.bfloat16), pltpu.HBM(raw.shape, jnp.bfloat16)],
        scratch_shapes=[pltpu.VMEM((block, channels), jnp.float32)],
        compiler_params=pltpu.CompilerParams(vmem_limit_bytes=VMEM_LIMIT),
        cost_estimate=COST,
        name="cross_own",
    )(raw, summed)


def cross_next_kernel(count, group_ref, unit_ref, raw_ref, summed_ref, *refs):
    *out_refs, inv_ref, terms_ref = refs
    parts = len(out_refs)
    rows = raw_ref.shape[1] // parts

    @pl.when(pl.program_id(0) == 0)
    def _():
        inv_ref[...] = jnp.broadcast_to(inverse_norm(summed_ref[0:1, :], count), inv_ref.shape)

    inv_norm = inv_ref[...]
    at = [pl.multiple_of(rows * lax.rem(group_ref[0] + r, parts), rows) for r in range(parts)]
    for k in range(raw_ref.shape[0]):
        real, imag = pair_terms(unit_ref[k], normalized(raw_ref[k], inv_norm))
        terms_ref[k, 0] = real
        terms_ref[k, 1] = imag
    for k in range(raw_ref.shape[0]):
        for r in range(parts):
            for c in range(2):
                place = slice((2 * k + c) * rows, (2 * k + c + 1) * rows)
                out_refs[r][place, :] = terms_ref[k, c, pl.ds(at[r], rows), :].astype(jnp.bfloat16)


def cross_next(group_index, unit, raw, summed, parts, steps):
    freq, block, channels = raw.shape
    rows = freq * 2 * block // parts
    one = freq // steps
    spec = pl.BlockSpec((one, block, channels), lambda s, g: (s, 0, 0))
    return pl.pallas_call(
        functools.partial(cross_next_kernel, freq * parts * channels),
        grid_spec=pltpu.PrefetchScalarGridSpec(
            num_scalar_prefetch=1,
            grid=(steps,),
            in_specs=[spec, spec, pl.BlockSpec(summed.shape, lambda s, g: (0, 0))],
            out_specs=[pl.BlockSpec((rows // steps, block), lambda s, g: (s, 0))] * parts,
            scratch_shapes=[
                pltpu.VMEM((block, channels), jnp.float32),
                pltpu.VMEM((one, 2, block, block), jnp.float32),
            ],
        ),
        out_shape=[pltpu.HBM((rows, block), jnp.bfloat16)] * parts,
        compiler_params=pltpu.CompilerParams(vmem_limit_bytes=VMEM_LIMIT),
        cost_estimate=COST,
        name="cross_next",
    )(group_index, unit, raw, summed)


def turn(load, pieces, piece_rows, held_ref, base, width, rows, block):
    chunk = 16 * rows
    at = iota((chunk, chunk), 0)
    matrix = (iota((chunk, chunk), 1) == (at & 15) * rows + (at >> 4)).astype(jnp.bfloat16)
    total = pieces * piece_rows
    for c in range(-(-total // chunk)):
        begin, end = c * chunk, min((c + 1) * chunk, total)
        found = []
        for p in range(begin // piece_rows, (end - 1) // piece_rows + 1):
            low, high = max(begin, p * piece_rows), min(end, (p + 1) * piece_rows)
            found.append(load(p, low - p * piece_rows, high - low))
        piece = found[0] if len(found) == 1 else jnp.concatenate(found, axis=0)
        turned = jnp.dot(matrix[:, : end - begin], piece, preferred_element_type=jnp.float32).astype(jnp.bfloat16)
        for i in range(rows):
            held_ref[base + c * 16 : base + (c + 1) * 16, i * block : (i + 1) * block] = turned[i * 16 : (i + 1) * 16]
    used = -(-total // chunk) * 16
    if used < width:
        held_ref[base + used : base + width, :] = jnp.zeros((width - used, rows * block), jnp.bfloat16)


def mean_exp(corr, factor):
    return jnp.sum(jnp.exp(factor * corr), axis=0, keepdims=True) * (1.0 / corr.shape[0])


def own_kernel(factor, group_ref, terms_ref, trig_ref, out_ref, held_ref):
    parts, size, block = terms_ref.shape
    rows = out_ref.shape[0]
    sources = [lax.rem(group_ref[0] + (parts - p), parts) for p in range(parts)]

    def load(p, begin, count):
        return terms_ref[sources[p], begin : begin + count, :]

    half = parts // 2
    width = trig_ref.shape[1] // 2
    for h in range(2):
        turn(lambda p, *where: load(h * half + p, *where), half, size, held_ref, h * width, width, rows, block)
    for i in range(0, rows, 2):
        corr = jnp.dot(trig_ref[...], held_ref[:, i * block : (i + 2) * block], preferred_element_type=jnp.float32)
        mean = mean_exp(corr, factor)
        out_ref[i : i + 1, :] = mean[:, :block]
        out_ref[i + 1 : i + 2, :] = mean[:, block:]
    at = iota((rows, block), 0) + rows * group_ref[0]
    gap = (iota((rows, block), 1) - at) & (block - 1)
    out_ref[...] = jnp.where(gap == 0, 0.0, out_ref[...])


def own_part(group_index, terms, trig, factor):
    parts, _, block = terms.shape
    rows = block // 2 // parts
    return pl.pallas_call(
        functools.partial(own_kernel, factor),
        in_specs=[pl.BlockSpec(memory_space=pltpu.SMEM)] + [pl.BlockSpec(memory_space=pltpu.VMEM)] * 2,
        out_specs=pl.BlockSpec(memory_space=pltpu.VMEM),
        out_shape=jax.ShapeDtypeStruct((rows, block), jnp.float32),
        scratch_shapes=[pltpu.VMEM((trig.shape[1], rows * block), jnp.bfloat16)],
        compiler_params=pltpu.CompilerParams(vmem_limit_bytes=VMEM_LIMIT),
        name="own_part",
    )(group_index, terms, trig)


def first_kernel(trig_ref, *refs):
    *piece_refs, out_ref, held_ref = refs
    rows = 16
    size, block = piece_refs[0].shape
    width = held_ref.shape[0]
    turn(lambda p, b, n: piece_refs[p][b : b + n, :], len(piece_refs), size, held_ref, 0, width, rows, block)
    for i in range(0, rows, 2):
        cut = slice(i * block, (i + 2) * block)
        out_ref[:, cut] = jnp.dot(trig_ref[:, :width], held_ref[:, cut], preferred_element_type=jnp.float32)


def first_part(pieces, trig):
    rows = 16
    block = pieces[0].shape[1]
    return pl.pallas_call(
        first_kernel,
        in_specs=[pl.BlockSpec(memory_space=pltpu.VMEM)] * (1 + len(pieces)),
        out_specs=pl.BlockSpec(memory_space=pltpu.VMEM),
        out_shape=jax.ShapeDtypeStruct((trig.shape[0], rows * block), jnp.float32),
        scratch_shapes=[pltpu.VMEM((trig.shape[1] // 2, rows * block), jnp.bfloat16)],
        compiler_params=pltpu.CompilerParams(vmem_limit_bytes=VMEM_LIMIT),
        name="first_part",
    )(trig, *pieces)


def next_kernel(factor, group_ref, trig_ref, own_ref, summed_ref, share_ref, *refs):
    *piece_refs, out_ref, held_ref, wide_ref = refs
    rows = 16
    size, block = piece_refs[0].shape
    half = block // 2
    group = group_ref[0]
    width = held_ref.shape[0]
    turn(lambda p, b, n: piece_refs[p][b : b + n, :], len(piece_refs), size, held_ref, 0, width, rows, block)
    for i in range(0, rows, 2):
        cut = slice(i * block, (i + 2) * block)
        corr = jnp.dot(trig_ref[:, width:], held_ref[:, cut], preferred_element_type=jnp.float32)
        mean = mean_exp(share_ref[:, cut] + corr, factor)
        out_ref[i : i + 1, :] = mean[:, :block]
        out_ref[i + 1 : i + 2, :] = mean[:, block:]
    own = own_ref[...]
    at = iota((8, block), 0) + 8 * group
    gap = (iota((8, block), 1) - at) & (block - 1)
    top = (gap >= 1) & (gap <= half)
    upper, lower = jnp.where(top, own, 0.0), jnp.where(top, 0.0, own)
    wide_ref[...] = jnp.zeros_like(wide_ref)
    wide_ref[pl.ds(pl.multiple_of(rows * group, rows), rows), :] = out_ref[0:rows, :]
    own_at = pl.multiple_of(8 * group, 8)
    wide_ref[pl.ds(block + own_at, 8), :] = upper
    wide_ref[pl.ds(block + half + own_at, 8), :] = lower
    ones = jnp.ones((8, block), jnp.float32)
    by_row = dot(ones, wide_ref[...], ((1,), (1,)))
    degree = by_row[0:1, :block] + by_row[0:1, block:] + jnp.sum(own, axis=0, keepdims=True)
    out_ref[rows : rows + 8, :] = jnp.zeros((8, block), jnp.float32)
    out_ref[rows : rows + 1, :] = degree
    out_ref[rows + 1 : rows + 2, :] = jnp.sum(out_ref[0:rows, :], axis=0, keepdims=True)
    out_ref[rows + 8 :, :] = summed_ref[8:, :]


def next_part(group_index, share, pieces, trig, own, summed, factor):
    rows = 16
    block = pieces[0].shape[1]
    return pl.pallas_call(
        functools.partial(next_kernel, factor),
        in_specs=[pl.BlockSpec(memory_space=pltpu.SMEM)]
        + [pl.BlockSpec(memory_space=pltpu.VMEM)] * (4 + len(pieces)),
        out_specs=pl.BlockSpec(memory_space=pltpu.VMEM),
        out_shape=jax.ShapeDtypeStruct((rows + summed.shape[0], block), jnp.float32),
        scratch_shapes=[
            pltpu.VMEM((trig.shape[1] // 2, rows * block), jnp.bfloat16),
            pltpu.VMEM((2 * block, block), jnp.float32),
        ],
        compiler_params=pltpu.CompilerParams(vmem_limit_bytes=VMEM_LIMIT),
        name="next_part",
    )(group_index, trig, own, summed, share, *pieces)


def image_kernel(group_ref, parts_ref, before_ref, here_ref, after_ref, out_ref, own_ref, full_ref):
    groups, _, block = parts_ref.shape
    half = block // 2
    shares = parts_ref[0, 40:48, :]
    for s in range(groups):
        if s:
            shares = shares + parts_ref[s, 40:48, :]
        full_ref[0, 16 * s : 16 * s + 16, :] = parts_ref[s, 0:16, :]
        full_ref[1, 16 * s : 16 * s + 16, :] = parts_ref[s, 16:32, :]
        full_ref[2, 8 * s : 8 * s + 8, :] = parts_ref[s, 32:40, :]
    top = upper_half(half, block)
    own = full_ref[2, 0:half, :]
    full_ref[2, 0:half, :] = jnp.where(top, own, 0.0)
    full_ref[2, half:block, :] = jnp.where(top, 0.0, own)
    inv_root = lax.rsqrt(shares)
    scaled_before = before_ref[24:, :] * inv_root[0:1, :]
    scaled_own = here_ref[8:, :] * inv_root[1:2, :]
    scaled_after = after_ref[8:, :] * inv_root[2:3, :]
    along, across = ((1,), (1,)), ((1,), (0,))
    product = dot(scaled_own, full_ref[2], along) + dot(scaled_own, full_ref[2], across)
    product = product + dot(scaled_after, full_ref[0], along) + dot(scaled_before, full_ref[1], across)
    image = product * inv_root[1:2, :] * (3.0 * block)
    degree = shares[1:2, :]
    root_degree = jnp.sqrt(degree)
    degree_sum = jnp.sum(degree, axis=1, keepdims=True)
    proj = jnp.sum(root_degree * image, axis=1, keepdims=True)
    rest = image - root_degree * (proj / degree_sum)
    rest_sq = jnp.sum(rest * rest, axis=1, keepdims=True)
    count = image.shape[0]
    at, lane = iota((count, block), 0), iota((count, block), 1)
    stats = jnp.where(lane == at, proj, 0.0) + jnp.where(lane == at + count, rest_sq, 0.0)
    stats = jnp.sum(stats, axis=0, keepdims=True)
    stats = jnp.where(iota((1, block), 1) == 2 * count, degree_sum, stats)
    out_ref[...] = jnp.broadcast_to(stats, out_ref.shape)
    place = (lane == at + count * group_ref[0]).astype(jnp.float32)
    own_ref[0] = dot(place, image, along)
    own_ref[1] = dot(place, jnp.broadcast_to(root_degree, image.shape), along)


def image_part(group_index, parts, before, here, after, n_blk):
    groups, _, block = parts.shape
    count = here.shape[0] - 8
    return pl.pallas_call(
        image_kernel,
        in_specs=[pl.BlockSpec(memory_space=pltpu.SMEM)] + [pl.BlockSpec(memory_space=pltpu.VMEM)] * 4,
        out_specs=[pl.BlockSpec(memory_space=pltpu.VMEM)] * 2,
        out_shape=[
            jax.ShapeDtypeStruct((n_blk, block), jnp.float32),
            jax.ShapeDtypeStruct((2, count, count), jnp.float32),
        ],
        scratch_shapes=[pltpu.VMEM((3, block, block), jnp.float32)],
        compiler_params=pltpu.CompilerParams(vmem_limit_bytes=VMEM_LIMIT),
        name="image_part",
    )(group_index, parts, before, here, after)


def final_kernel(total_rows, stats_ref, own_ref, out_ref):
    count = out_ref.shape[1]
    stats = stats_ref[...]
    proj, rest_sq, degree = stats[:, :count], stats[:, count : 2 * count], stats[:, 2 * count : 2 * count + 1]
    ratio = jnp.sum(proj, axis=0, keepdims=True) / jnp.sum(degree, axis=0, keepdims=True)
    shift = proj / degree - ratio
    column_sq = jnp.sum(rest_sq + degree * (shift * shift), axis=0, keepdims=True)
    deflated = own_ref[0] - own_ref[1] * ratio
    out_ref[...] = deflated * lax.rsqrt(column_sq / total_rows + epsilon)


def final_part(stats, own, total_rows):
    count = own.shape[1]
    return pl.pallas_call(
        functools.partial(final_kernel, total_rows),
        in_specs=[pl.BlockSpec(memory_space=pltpu.VMEM)] * 2,
        out_specs=pl.BlockSpec(memory_space=pltpu.VMEM),
        out_shape=jax.ShapeDtypeStruct((count, count), jnp.float32),
        name="final_part",
    )(stats, own)


def per_device(coeffs, vectors):
    block, freq_local, channels = coeffs.shape
    group_size = lax.axis_size("grp")
    n_blk = lax.axis_size("blk")
    group_index = lax.axis_index("grp").astype(jnp.int32)[None]
    angles = freq_local * group_size
    factor = sharpness / math.sqrt(angles * channels)
    trig = trig_columns(freq_local, group_size, group_index[0])

    begun, by_freq = start(group_index, coeffs.transpose(1, 0, 2), vectors, group_size)
    summed = jnp.sum(lax.all_to_all(begun, "grp", 0, 0, tiled=True), axis=0)
    after_raw = passed_along(by_freq, "blk", -1)
    summed_after = passed_along(summed, "blk", -1)
    own_terms, own_unit = cross_own(by_freq, summed, group_size, 5)
    own_terms = lax.all_to_all(own_terms, "grp", 0, 0, tiled=True)
    next_terms = cross_next(group_index, own_unit, after_raw, summed_after, group_size, 5)
    next_terms = [next_terms[0]] + [passed_along(next_terms[r], "grp", r) for r in range(1, group_size)]
    own_aff = own_part(group_index, own_terms, trig, factor)
    share = first_part(next_terms[: group_size // 2], trig)
    found = next_part(group_index, share, next_terms[group_size // 2 :], trig, own_aff, summed, factor)

    found_before = passed_along(found, "blk", 1)
    edge_after = passed_along(found[16:24], "blk", -1)
    edge_before = passed_along(found[16:24], "blk", 2)
    zeros = jnp.zeros((5, block), jnp.float32)
    shares = jnp.concatenate(
        [
            found_before[16:17] + edge_before[1:2],
            found[16:17] + found_before[17:18],
            edge_after[0:1] + found[17:18],
            zeros,
        ],
        axis=0,
    )
    sent = jnp.concatenate([found[:16], found_before[:16], own_aff, shares], axis=0)
    sent = jnp.broadcast_to(sent[None], (group_size,) + sent.shape)
    parts = lax.all_to_all(sent, "grp", 0, 0, tiled=True)
    stats, own = image_part(group_index, parts, found_before, summed, summed_after, n_blk)
    stats = lax.all_to_all(stats, "blk", 0, 0, tiled=True)
    return final_part(stats, own, block * n_blk)


def solution(mesh):
    placed = (P("blk", "grp", None), P(("blk", "grp"), None))
    return jax.shard_map(
        per_device, mesh=mesh, in_specs=placed, out_specs=P(("blk", "grp"), None), check_vma=False
    )
```

```python
import functools
import math

import jax
import jax.numpy as jnp
from jax import lax
from jax.experimental import pallas as pl
from jax.experimental.pallas import tpu as pltpu
from jax.sharding import PartitionSpec as P

sharpness = 2.5
epsilon = 1e-06
HIGHEST = lax.Precision.HIGHEST
COST = pl.CostEstimate(flops=20000000000, transcendentals=0, bytes_accessed=6_000_000)
VMEM_LIMIT = 24 * 1024 * 1024


def passed_along(block, axis, distance):
    devices = range(lax.axis_size(axis))
    route = [((i - distance) % len(devices), i) for i in devices]
    return lax.ppermute(block, axis, route)


def trig_columns(freq_local, group_size, group_index):
    total = freq_local * group_size
    half_width = (total + 127) // 128 * 128
    column = jnp.arange(2 * half_width, dtype=jnp.int32)
    place = column // half_width * total + column % half_width
    within = place % (2 * freq_local)
    source = (group_index + group_size - place // (2 * freq_local) % group_size) % group_size
    freq = source * freq_local + within // 2
    angles = jnp.arange(total, dtype=jnp.int32)
    phase = (angles[:, None] * freq[None, :] % total).astype(jnp.float32) * (2.0 * math.pi / total)
    cos_part = jnp.cos(phase).astype(jnp.bfloat16)
    sin_part = (-jnp.sin(phase)).astype(jnp.bfloat16)
    found = jnp.where((within % 2 == 1)[None, :], sin_part, cos_part)
    return jnp.where((column % half_width < total)[None, :], found, jnp.zeros_like(found))


def iota(shape, dim):
    return lax.broadcasted_iota(jnp.int32, shape, dim)


def dot(a, b, dims):
    return lax.dot_general(a, b, (dims, ((), ())), precision=HIGHEST, preferred_element_type=jnp.float32)


def start_kernel(group_ref, coeffs_ref, vectors_ref, out_ref, same_ref, sq_ref):
    step = pl.program_id(0)

    @pl.when(step == 0)
    def _():
        sq_ref[...] = jnp.zeros_like(sq_ref)

    total = sq_ref[...]
    for k in range(coeffs_ref.shape[0]):
        values = coeffs_ref[k].astype(jnp.float32)
        total = total + values * values
    sq_ref[...] = total
    same_ref[...] = coeffs_ref[...]

    @pl.when(step == pl.num_programs(0) - 1)
    def _():
        block = sq_ref.shape[0]
        rows = vectors_ref.shape[0]
        total = dot(jnp.ones((8, sq_ref.shape[1]), jnp.float32), sq_ref[...], ((1,), (1,)))
        place = iota((rows, block), 1) == iota((rows, block), 0) + rows * group_ref[0]
        placed = dot(vectors_ref[...], place.astype(jnp.float32), ((0,), (0,)))
        for d in range(out_ref.shape[0]):
            out_ref[d, 0:8, :] = total
            out_ref[d, 8 : 8 + placed.shape[0], :] = placed


def start(group_index, coeffs, vectors, group_size):
    freq_local, block, channels = coeffs.shape
    rows = 8 + vectors.shape[1]
    steps = 3
    return pl.pallas_call(
        start_kernel,
        grid_spec=pltpu.PrefetchScalarGridSpec(
            num_scalar_prefetch=1,
            grid=(steps,),
            in_specs=[
                pl.BlockSpec((freq_local // steps, block, channels), lambda s, g: (s, 0, 0)),
                pl.BlockSpec(vectors.shape, lambda s, g: (0, 0)),
            ],
            out_specs=[
                pl.BlockSpec((group_size, rows, block), lambda s, g: (0, 0, 0)),
                pl.BlockSpec((freq_local // steps, block, channels), lambda s, g: (s, 0, 0)),
            ],
            scratch_shapes=[pltpu.VMEM((block, channels), jnp.float32)],
        ),
        out_shape=[pltpu.HBM((group_size, rows, block), jnp.float32), pltpu.HBM(coeffs.shape, coeffs.dtype)],
        compiler_params=pltpu.CompilerParams(vmem_limit_bytes=VMEM_LIMIT),
        name="start",
    )(group_index, coeffs, vectors)


def swapped(a):
    half = a.shape[1] // 2
    wide = a.astype(jnp.float32)
    turned = pltpu.roll(wide, half, 1)
    return jnp.where(iota(a.shape, 1) < half, turned, -turned).astype(a.dtype)


def upper_half(half, block):
    gap = (iota((half, block), 1) - iota((half, block), 0)) & (block - 1)
    return (gap >= 1) & (gap <= half)


def inverse_norm(total, count):
    block = total.shape[1]
    eye = iota((block, block), 0) == iota((block, block), 1)
    column = jnp.sum(jnp.where(eye, total, 0.0), axis=1, keepdims=True)
    return lax.rsqrt(column / count + epsilon)


def normalized(raw, inv_norm):
    return (raw.astype(jnp.float32) * inv_norm).astype(jnp.bfloat16)


def pair_terms(own, other):
    lhs = jnp.concatenate([own, swapped(own)], axis=0)
    pair = lax.dot_general(lhs, other, (((1,), (1,)), ((), ())), preferred_element_type=jnp.float32)
    return pair[: own.shape[0]], pair[own.shape[0] :]


def store_terms(out_ref, k, real, imag):
    parts = out_ref.shape[0]
    rows = real.shape[0] // parts
    for d in range(parts):
        both = jnp.concatenate([real[d * rows : (d + 1) * rows], imag[d * rows : (d + 1) * rows]], axis=0)
        out_ref[d, k * 2 * rows : (k + 1) * 2 * rows, :] = both.astype(jnp.bfloat16)


def cross_own_kernel(count, raw_ref, summed_ref, out_ref, unit_ref, inv_ref):
    block = raw_ref.shape[1]
    half = block // 2

    @pl.when(pl.program_id(0) == 0)
    def _():
        inv_ref[...] = jnp.broadcast_to(inverse_norm(summed_ref[0:1, :], count), inv_ref.shape)

    inv_norm = inv_ref[...]
    top = upper_half(half, block)
    for k in range(raw_ref.shape[0]):
        unit = normalized(raw_ref[k], inv_norm)
        unit_ref[k] = unit
        real, imag = pair_terms(unit, unit)
        store_terms(out_ref, k, jnp.where(top, real[:half], real[half:]), jnp.where(top, imag[:half], imag[half:]))


def cross_own(raw, summed, parts, steps):
    freq, block, channels = raw.shape
    rows = freq * block // parts
    spec = pl.BlockSpec((freq // steps, block, channels), lambda s: (s, 0, 0))
    return pl.pallas_call(
        functools.partial(cross_own_kernel, freq * parts * channels),
        grid=(steps,),
        in_specs=[spec, pl.BlockSpec(summed.shape, lambda s: (0, 0))],
        out_specs=[pl.BlockSpec((parts, rows // steps, block), lambda s: (0, s, 0)), spec],
        out_shape=[pltpu.HBM((parts, rows, block), jnp.bfloat16), pltpu.HBM(raw.shape, jnp.bfloat16)],
        scratch_shapes=[pltpu.VMEM((block, channels), jnp.float32)],
        compiler_params=pltpu.CompilerParams(vmem_limit_bytes=VMEM_LIMIT),
        cost_estimate=COST,
        name="cross_own",
    )(raw, summed)


def cross_next_kernel(count, group_ref, unit_ref, raw_ref, summed_ref, *refs):
    *out_refs, inv_ref, terms_ref = refs
    parts = len(out_refs)
    rows = raw_ref.shape[1] // parts

    @pl.when(pl.program_id(0) == 0)
    def _():
        inv_ref[...] = jnp.broadcast_to(inverse_norm(summed_ref[0:1, :], count), inv_ref.shape)

    inv_norm = inv_ref[...]
    at = [pl.multiple_of(rows * lax.rem(group_ref[0] + r, parts), rows) for r in range(parts)]
    for k in range(raw_ref.shape[0]):
        real, imag = pair_terms(unit_ref[k], normalized(raw_ref[k], inv_norm))
        terms_ref[k, 0] = real
        terms_ref[k, 1] = imag
    for k in range(raw_ref.shape[0]):
        for r in range(parts):
            for c in range(2):
                place = slice((2 * k + c) * rows, (2 * k + c + 1) * rows)
                out_refs[r][place, :] = terms_ref[k, c, pl.ds(at[r], rows), :].astype(jnp.bfloat16)


def cross_next(group_index, unit, raw, summed, parts, steps):
    freq, block, channels = raw.shape
    rows = freq * 2 * block // parts
    one = freq // steps
    spec = pl.BlockSpec((one, block, channels), lambda s, g: (s, 0, 0))
    return pl.pallas_call(
        functools.partial(cross_next_kernel, freq * parts * channels),
        grid_spec=pltpu.PrefetchScalarGridSpec(
            num_scalar_prefetch=1,
            grid=(steps,),
            in_specs=[spec, spec, pl.BlockSpec(summed.shape, lambda s, g: (0, 0))],
            out_specs=[pl.BlockSpec((rows // steps, block), lambda s, g: (s, 0))] * parts,
            scratch_shapes=[
                pltpu.VMEM((block, channels), jnp.float32),
                pltpu.VMEM((one, 2, block, block), jnp.float32),
            ],
        ),
        out_shape=[pltpu.HBM((rows, block), jnp.bfloat16)] * parts,
        compiler_params=pltpu.CompilerParams(vmem_limit_bytes=VMEM_LIMIT),
        cost_estimate=COST,
        name="cross_next",
    )(group_index, unit, raw, summed)


def turn(load, pieces, piece_rows, held_ref, base, width, rows, block):
    chunk = 16 * rows
    at = iota((chunk, chunk), 0)
    matrix = (iota((chunk, chunk), 1) == (at & 15) * rows + (at >> 4)).astype(jnp.bfloat16)
    total = pieces * piece_rows
    for c in range(-(-total // chunk)):
        begin, end = c * chunk, min((c + 1) * chunk, total)
        found = []
        for p in range(begin // piece_rows, (end - 1) // piece_rows + 1):
            low, high = max(begin, p * piece_rows), min(end, (p + 1) * piece_rows)
            found.append(load(p, low - p * piece_rows, high - low))
        piece = found[0] if len(found) == 1 else jnp.concatenate(found, axis=0)
        turned = jnp.dot(matrix[:, : end - begin], piece, preferred_element_type=jnp.float32).astype(jnp.bfloat16)
        for i in range(rows):
            held_ref[base + c * 16 : base + (c + 1) * 16, i * block : (i + 1) * block] = turned[i * 16 : (i + 1) * 16]
    used = -(-total // chunk) * 16
    if used < width:
        held_ref[base + used : base + width, :] = jnp.zeros((width - used, rows * block), jnp.bfloat16)


def mean_exp(corr, factor):
    return jnp.sum(jnp.exp(factor * corr), axis=0, keepdims=True) * (1.0 / corr.shape[0])


def own_kernel(factor, group_ref, terms_ref, trig_ref, out_ref, degree_ref, held_ref, wide_ref):
    parts, size, block = terms_ref.shape
    rows = out_ref.shape[0]
    sources = [lax.rem(group_ref[0] + (parts - p), parts) for p in range(parts)]

    def load(p, begin, count):
        return terms_ref[sources[p], begin : begin + count, :]

    half = parts // 2
    width = trig_ref.shape[1] // 2
    for h in range(2):
        turn(lambda p, *where: load(h * half + p, *where), half, size, held_ref, h * width, width, rows, block)
    for i in range(0, rows, 2):
        corr = jnp.dot(trig_ref[...], held_ref[:, i * block : (i + 2) * block], preferred_element_type=jnp.float32)
        mean = mean_exp(corr, factor)
        out_ref[i : i + 1, :] = mean[:, :block]
        out_ref[i + 1 : i + 2, :] = mean[:, block:]
    at = iota((rows, block), 0) + rows * group_ref[0]
    gap = (iota((rows, block), 1) - at) & (block - 1)
    own = jnp.where(gap == 0, 0.0, out_ref[...])
    out_ref[...] = own
    top = (gap >= 1) & (gap <= block // 2)
    own_at = pl.multiple_of(rows * group_ref[0], rows)
    wide_ref[...] = jnp.zeros_like(wide_ref)
    wide_ref[pl.ds(own_at, rows), :] = jnp.where(top, own, 0.0)
    wide_ref[pl.ds(block // 2 + own_at, rows), :] = jnp.where(top, 0.0, own)
    by_row = dot(jnp.ones((8, block), jnp.float32), wide_ref[...], ((1,), (1,)))
    degree_ref[...] = by_row[0:1] + jnp.sum(own, axis=0, keepdims=True)


def own_part(group_index, terms, trig, factor):
    parts, _, block = terms.shape
    rows = block // 2 // parts
    return pl.pallas_call(
        functools.partial(own_kernel, factor),
        in_specs=[pl.BlockSpec(memory_space=pltpu.SMEM)] + [pl.BlockSpec(memory_space=pltpu.VMEM)] * 2,
        out_specs=[pl.BlockSpec(memory_space=pltpu.VMEM)] * 2,
        out_shape=[jax.ShapeDtypeStruct((n, block), jnp.float32) for n in (rows, 1)],
        scratch_shapes=[
            pltpu.VMEM((trig.shape[1], rows * block), jnp.bfloat16),
            pltpu.VMEM((block, block), jnp.float32),
        ],
        compiler_params=pltpu.CompilerParams(vmem_limit_bytes=VMEM_LIMIT),
        name="own_part",
    )(group_index, terms, trig)


def first_kernel(trig_ref, *refs):
    *piece_refs, out_ref, held_ref = refs
    rows = 16
    size, block = piece_refs[0].shape
    width = held_ref.shape[0]
    turn(lambda p, b, n: piece_refs[p][b : b + n, :], len(piece_refs), size, held_ref, 0, width, rows, block)
    for i in range(0, rows, 2):
        cut = slice(i * block, (i + 2) * block)
        out_ref[:, cut] = jnp.dot(trig_ref[:, :width], held_ref[:, cut], preferred_element_type=jnp.float32)


def first_part(pieces, trig):
    rows = 16
    block = pieces[0].shape[1]
    return pl.pallas_call(
        first_kernel,
        in_specs=[pl.BlockSpec(memory_space=pltpu.VMEM)] * (1 + len(pieces)),
        out_specs=pl.BlockSpec(memory_space=pltpu.VMEM),
        out_shape=jax.ShapeDtypeStruct((trig.shape[0], rows * block), jnp.float32),
        scratch_shapes=[pltpu.VMEM((trig.shape[1] // 2, rows * block), jnp.bfloat16)],
        compiler_params=pltpu.CompilerParams(vmem_limit_bytes=VMEM_LIMIT),
        name="first_part",
    )(trig, *pieces)


def next_kernel(factor, group_ref, trig_ref, degree_ref, summed_ref, share_ref, *refs):
    *piece_refs, out_ref, held_ref, wide_ref = refs
    rows = 16
    size, block = piece_refs[0].shape
    group = group_ref[0]
    width = held_ref.shape[0]
    turn(lambda p, b, n: piece_refs[p][b : b + n, :], len(piece_refs), size, held_ref, 0, width, rows, block)
    for i in range(0, rows, 2):
        cut = slice(i * block, (i + 2) * block)
        corr = jnp.dot(trig_ref[:, width:], held_ref[:, cut], preferred_element_type=jnp.float32)
        mean = mean_exp(share_ref[:, cut] + corr, factor)
        out_ref[i : i + 1, :] = mean[:, :block]
        out_ref[i + 1 : i + 2, :] = mean[:, block:]
    wide_ref[...] = jnp.zeros_like(wide_ref)
    wide_ref[pl.ds(pl.multiple_of(rows * group, rows), rows), :] = out_ref[0:rows, :]
    ones = jnp.ones((8, block), jnp.float32)
    by_row = dot(ones, wide_ref[...], ((1,), (1,)))
    degree = by_row[0:1] + degree_ref[...]
    out_ref[rows : rows + 8, :] = jnp.zeros((8, block), jnp.float32)
    out_ref[rows : rows + 1, :] = degree
    out_ref[rows + 1 : rows + 2, :] = jnp.sum(out_ref[0:rows, :], axis=0, keepdims=True)
    out_ref[rows + 8 :, :] = summed_ref[8:, :]


def next_part(group_index, share, pieces, trig, own_degree, summed, factor):
    rows = 16
    block = pieces[0].shape[1]
    return pl.pallas_call(
        functools.partial(next_kernel, factor),
        in_specs=[pl.BlockSpec(memory_space=pltpu.SMEM)]
        + [pl.BlockSpec(memory_space=pltpu.VMEM)] * (4 + len(pieces)),
        out_specs=pl.BlockSpec(memory_space=pltpu.VMEM),
        out_shape=jax.ShapeDtypeStruct((rows + summed.shape[0], block), jnp.float32),
        scratch_shapes=[
            pltpu.VMEM((trig.shape[1] // 2, rows * block), jnp.bfloat16),
            pltpu.VMEM((block, block), jnp.float32),
        ],
        compiler_params=pltpu.CompilerParams(vmem_limit_bytes=VMEM_LIMIT),
        name="next_part",
    )(group_index, trig, own_degree, summed, share, *pieces)


def image_kernel(group_ref, parts_ref, before_ref, here_ref, after_ref, out_ref, own_ref, full_ref):
    groups, _, block = parts_ref.shape
    half = block // 2
    shares = parts_ref[0, 40:48, :]
    for s in range(groups):
        if s:
            shares = shares + parts_ref[s, 40:48, :]
        full_ref[0, 16 * s : 16 * s + 16, :] = parts_ref[s, 0:16, :]
        full_ref[1, 16 * s : 16 * s + 16, :] = parts_ref[s, 16:32, :]
        full_ref[2, 8 * s : 8 * s + 8, :] = parts_ref[s, 32:40, :]
    top = upper_half(half, block)
    own = full_ref[2, 0:half, :]
    full_ref[2, 0:half, :] = jnp.where(top, own, 0.0)
    full_ref[2, half:block, :] = jnp.where(top, 0.0, own)
    inv_root = lax.rsqrt(shares)
    scaled_before = before_ref[24:, :] * inv_root[0:1, :]
    scaled_own = here_ref[8:, :] * inv_root[1:2, :]
    scaled_after = after_ref[8:, :] * inv_root[2:3, :]
    along, across = ((1,), (1,)), ((1,), (0,))
    product = dot(scaled_own, full_ref[2], along) + dot(scaled_own, full_ref[2], across)
    product = product + dot(scaled_after, full_ref[0], along) + dot(scaled_before, full_ref[1], across)
    image = product * inv_root[1:2, :] * (3.0 * block)
    degree = shares[1:2, :]
    root_degree = jnp.sqrt(degree)
    degree_sum = jnp.sum(degree, axis=1, keepdims=True)
    proj = jnp.sum(root_degree * image, axis=1, keepdims=True)
    rest = image - root_degree * (proj / degree_sum)
    rest_sq = jnp.sum(rest * rest, axis=1, keepdims=True)
    count = image.shape[0]
    at, lane = iota((count, block), 0), iota((count, block), 1)
    stats = jnp.where(lane == at, proj, 0.0) + jnp.where(lane == at + count, rest_sq, 0.0)
    stats = jnp.sum(stats, axis=0, keepdims=True)
    stats = jnp.where(iota((1, block), 1) == 2 * count, degree_sum, stats)
    out_ref[...] = jnp.broadcast_to(stats, out_ref.shape)
    place = (lane == at + count * group_ref[0]).astype(jnp.float32)
    own_ref[0] = dot(place, image, along)
    own_ref[1] = dot(place, jnp.broadcast_to(root_degree, image.shape), along)


def image_part(group_index, parts, before, here, after, n_blk):
    groups, _, block = parts.shape
    count = here.shape[0] - 8
    return pl.pallas_call(
        image_kernel,
        in_specs=[pl.BlockSpec(memory_space=pltpu.SMEM)] + [pl.BlockSpec(memory_space=pltpu.VMEM)] * 4,
        out_specs=[pl.BlockSpec(memory_space=pltpu.VMEM)] * 2,
        out_shape=[
            jax.ShapeDtypeStruct((n_blk, block), jnp.float32),
            jax.ShapeDtypeStruct((2, count, count), jnp.float32),
        ],
        scratch_shapes=[pltpu.VMEM((3, block, block), jnp.float32)],
        compiler_params=pltpu.CompilerParams(vmem_limit_bytes=VMEM_LIMIT),
        name="image_part",
    )(group_index, parts, before, here, after)


def final_kernel(total_rows, stats_ref, own_ref, out_ref):
    count = out_ref.shape[1]
    stats = stats_ref[...]
    proj, rest_sq, degree = stats[:, :count], stats[:, count : 2 * count], stats[:, 2 * count : 2 * count + 1]
    ratio = jnp.sum(proj, axis=0, keepdims=True) / jnp.sum(degree, axis=0, keepdims=True)
    shift = proj / degree - ratio
    column_sq = jnp.sum(rest_sq + degree * (shift * shift), axis=0, keepdims=True)
    deflated = own_ref[0] - own_ref[1] * ratio
    out_ref[...] = deflated * lax.rsqrt(column_sq / total_rows + epsilon)


def final_part(stats, own, total_rows):
    count = own.shape[1]
    return pl.pallas_call(
        functools.partial(final_kernel, total_rows),
        in_specs=[pl.BlockSpec(memory_space=pltpu.VMEM)] * 2,
        out_specs=pl.BlockSpec(memory_space=pltpu.VMEM),
        out_shape=jax.ShapeDtypeStruct((count, count), jnp.float32),
        name="final_part",
    )(stats, own)


def per_device(coeffs, vectors):
    block, freq_local, channels = coeffs.shape
    group_size = lax.axis_size("grp")
    n_blk = lax.axis_size("blk")
    group_index = lax.axis_index("grp").astype(jnp.int32)[None]
    angles = freq_local * group_size
    factor = sharpness / math.sqrt(angles * channels)
    trig = trig_columns(freq_local, group_size, group_index[0])

    begun, by_freq = start(group_index, coeffs.transpose(1, 0, 2), vectors, group_size)
    summed = jnp.sum(lax.all_to_all(begun, "grp", 0, 0, tiled=True), axis=0)
    after_raw = passed_along(by_freq, "blk", -1)
    summed_after = passed_along(summed, "blk", -1)
    own_terms, own_unit = cross_own(by_freq, summed, group_size, 5)
    own_terms = lax.all_to_all(own_terms, "grp", 0, 0, tiled=True)
    next_terms = cross_next(group_index, own_unit, after_raw, summed_after, group_size, 5)
    next_terms = [next_terms[0]] + [passed_along(next_terms[r], "grp", r) for r in range(1, group_size)]
    own_aff, own_degree = own_part(group_index, own_terms, trig, factor)
    share = first_part(next_terms[: group_size // 2], trig)
    found = next_part(group_index, share, next_terms[group_size // 2 :], trig, own_degree, summed, factor)

    found_before = passed_along(found, "blk", 1)
    edge_after = passed_along(found[16:24], "blk", -1)
    edge_before = passed_along(found[16:24], "blk", 2)
    zeros = jnp.zeros((5, block), jnp.float32)
    shares = jnp.concatenate(
        [
            found_before[16:17] + edge_before[1:2],
            found[16:17] + found_before[17:18],
            edge_after[0:1] + found[17:18],
            zeros,
        ],
        axis=0,
    )
    sent = jnp.concatenate([found[:16], found_before[:16], own_aff, shares], axis=0)
    sent = jnp.broadcast_to(sent[None], (group_size,) + sent.shape)
    parts = lax.all_to_all(sent, "grp", 0, 0, tiled=True)
    stats, own = image_part(group_index, parts, found_before, summed, summed_after, n_blk)
    stats = lax.all_to_all(stats, "blk", 0, 0, tiled=True)
    return final_part(stats, own, block * n_blk)


def solution(mesh):
    placed = (P("blk", "grp", None), P(("blk", "grp"), None))
    return jax.shard_map(
        per_device, mesh=mesh, in_specs=placed, out_specs=P(("blk", "grp"), None), check_vma=False
    )
```

```python
import functools
import math

import jax
import jax.numpy as jnp
from jax import lax
from jax.experimental import pallas as pl
from jax.experimental.pallas import tpu as pltpu
from jax.sharding import PartitionSpec as P

sharpness = 2.5
epsilon = 1e-06
HIGHEST = lax.Precision.HIGHEST
COST = pl.CostEstimate(flops=20000000000, transcendentals=0, bytes_accessed=6_000_000)
VMEM_LIMIT = 24 * 1024 * 1024


def passed_along(block, axis, distance):
    devices = range(lax.axis_size(axis))
    route = [((i - distance) % len(devices), i) for i in devices]
    return lax.ppermute(block, axis, route)


def trig_columns(freq_local, group_size, group_index):
    total = freq_local * group_size
    half_width = (total + 127) // 128 * 128
    column = jnp.arange(2 * half_width, dtype=jnp.int32)
    place = column // half_width * total + column % half_width
    within = place % (2 * freq_local)
    source = (group_index + group_size - place // (2 * freq_local) % group_size) % group_size
    freq = source * freq_local + within // 2
    angles = jnp.arange(total, dtype=jnp.int32)
    phase = (angles[:, None] * freq[None, :] % total).astype(jnp.float32) * (2.0 * math.pi / total)
    cos_part = jnp.cos(phase).astype(jnp.bfloat16)
    sin_part = (-jnp.sin(phase)).astype(jnp.bfloat16)
    found = jnp.where((within % 2 == 1)[None, :], sin_part, cos_part)
    return jnp.where((column % half_width < total)[None, :], found, jnp.zeros_like(found))


def iota(shape, dim):
    return lax.broadcasted_iota(jnp.int32, shape, dim)


def dot(a, b, dims):
    return lax.dot_general(a, b, (dims, ((), ())), precision=HIGHEST, preferred_element_type=jnp.float32)


def start_kernel(group_ref, coeffs_ref, vectors_ref, out_ref, same_ref, sq_ref):
    step = pl.program_id(0)

    @pl.when(step == 0)
    def _():
        sq_ref[...] = jnp.zeros_like(sq_ref)

    total = sq_ref[...]
    for k in range(coeffs_ref.shape[0]):
        values = coeffs_ref[k].astype(jnp.float32)
        total = total + values * values
    sq_ref[...] = total
    same_ref[...] = coeffs_ref[...]

    @pl.when(step == pl.num_programs(0) - 1)
    def _():
        block = sq_ref.shape[0]
        rows = vectors_ref.shape[0]
        total = dot(jnp.ones((8, sq_ref.shape[1]), jnp.float32), sq_ref[...], ((1,), (1,)))
        place = iota((rows, block), 1) == iota((rows, block), 0) + rows * group_ref[0]
        placed = dot(vectors_ref[...], place.astype(jnp.float32), ((0,), (0,)))
        for d in range(out_ref.shape[0]):
            out_ref[d, 0:8, :] = total
            out_ref[d, 8 : 8 + placed.shape[0], :] = placed


def start(group_index, coeffs, vectors, group_size):
    freq_local, block, channels = coeffs.shape
    rows = 8 + vectors.shape[1]
    steps = 3
    return pl.pallas_call(
        start_kernel,
        grid_spec=pltpu.PrefetchScalarGridSpec(
            num_scalar_prefetch=1,
            grid=(steps,),
            in_specs=[
                pl.BlockSpec((freq_local // steps, block, channels), lambda s, g: (s, 0, 0)),
                pl.BlockSpec(vectors.shape, lambda s, g: (0, 0)),
            ],
            out_specs=[
                pl.BlockSpec((group_size, rows, block), lambda s, g: (0, 0, 0)),
                pl.BlockSpec((freq_local // steps, block, channels), lambda s, g: (s, 0, 0)),
            ],
            scratch_shapes=[pltpu.VMEM((block, channels), jnp.float32)],
        ),
        out_shape=[pltpu.HBM((group_size, rows, block), jnp.float32), pltpu.HBM(coeffs.shape, coeffs.dtype)],
        compiler_params=pltpu.CompilerParams(vmem_limit_bytes=VMEM_LIMIT),
        name="start",
    )(group_index, coeffs, vectors)


def swapped(a):
    half = a.shape[1] // 2
    wide = a.astype(jnp.float32)
    turned = pltpu.roll(wide, half, 1)
    return jnp.where(iota(a.shape, 1) < half, turned, -turned).astype(a.dtype)


def upper_half(half, block):
    gap = (iota((half, block), 1) - iota((half, block), 0)) & (block - 1)
    return (gap >= 1) & (gap <= half)


def inverse_norm(total, count):
    block = total.shape[1]
    eye = iota((block, block), 0) == iota((block, block), 1)
    column = jnp.sum(jnp.where(eye, total, 0.0), axis=1, keepdims=True)
    return lax.rsqrt(column / count + epsilon)


def normalized(raw, inv_norm):
    return (raw.astype(jnp.float32) * inv_norm).astype(jnp.bfloat16)


def pair_terms(own, other):
    lhs = jnp.concatenate([own, swapped(own)], axis=0)
    pair = lax.dot_general(lhs, other, (((1,), (1,)), ((), ())), preferred_element_type=jnp.float32)
    return pair[: own.shape[0]], pair[own.shape[0] :]


def store_terms(out_ref, k, real, imag):
    parts = out_ref.shape[0]
    rows = real.shape[0] // parts
    for d in range(parts):
        both = jnp.concatenate([real[d * rows : (d + 1) * rows], imag[d * rows : (d + 1) * rows]], axis=0)
        out_ref[d, k * 2 * rows : (k + 1) * 2 * rows, :] = both.astype(jnp.bfloat16)


def cross_own_kernel(count, raw_ref, summed_ref, out_ref, unit_ref, inv_ref):
    block = raw_ref.shape[1]
    half = block // 2

    @pl.when(pl.program_id(0) == 0)
    def _():
        inv_ref[...] = jnp.broadcast_to(inverse_norm(summed_ref[0:1, :], count), inv_ref.shape)

    inv_norm = inv_ref[...]
    top = upper_half(half, block)
    for k in range(raw_ref.shape[0]):
        unit = normalized(raw_ref[k], inv_norm)
        unit_ref[k] = unit
        real, imag = pair_terms(unit, unit)
        store_terms(out_ref, k, jnp.where(top, real[:half], real[half:]), jnp.where(top, imag[:half], imag[half:]))


def cross_own(raw, summed, parts, steps):
    freq, block, channels = raw.shape
    rows = freq * block // parts
    spec = pl.BlockSpec((freq // steps, block, channels), lambda s: (s, 0, 0))
    return pl.pallas_call(
        functools.partial(cross_own_kernel, freq * parts * channels),
        grid=(steps,),
        in_specs=[spec, pl.BlockSpec(summed.shape, lambda s: (0, 0))],
        out_specs=[pl.BlockSpec((parts, rows // steps, block), lambda s: (0, s, 0)), spec],
        out_shape=[pltpu.HBM((parts, rows, block), jnp.bfloat16), pltpu.HBM(raw.shape, jnp.bfloat16)],
        scratch_shapes=[pltpu.VMEM((block, channels), jnp.float32)],
        compiler_params=pltpu.CompilerParams(vmem_limit_bytes=VMEM_LIMIT),
        cost_estimate=COST,
        name="cross_own",
    )(raw, summed)


def cross_next_kernel(count, group_ref, unit_ref, raw_ref, summed_ref, *refs):
    *out_refs, inv_ref, terms_ref = refs
    parts = len(out_refs)
    rows = raw_ref.shape[1] // parts

    @pl.when(pl.program_id(0) == 0)
    def _():
        inv_ref[...] = jnp.broadcast_to(inverse_norm(summed_ref[0:1, :], count), inv_ref.shape)

    inv_norm = inv_ref[...]
    at = [pl.multiple_of(rows * lax.rem(group_ref[0] + r, parts), rows) for r in range(parts)]
    for k in range(raw_ref.shape[0]):
        real, imag = pair_terms(unit_ref[k], normalized(raw_ref[k], inv_norm))
        terms_ref[k, 0] = real
        terms_ref[k, 1] = imag
    for k in range(raw_ref.shape[0]):
        for r in range(parts):
            for c in range(2):
                place = slice((2 * k + c) * rows, (2 * k + c + 1) * rows)
                out_refs[r][place, :] = terms_ref[k, c, pl.ds(at[r], rows), :].astype(jnp.bfloat16)


def cross_next(group_index, unit, raw, summed, parts, steps):
    freq, block, channels = raw.shape
    rows = freq * 2 * block // parts
    one = freq // steps
    spec = pl.BlockSpec((one, block, channels), lambda s, g: (s, 0, 0))
    return pl.pallas_call(
        functools.partial(cross_next_kernel, freq * parts * channels),
        grid_spec=pltpu.PrefetchScalarGridSpec(
            num_scalar_prefetch=1,
            grid=(steps,),
            in_specs=[spec, spec, pl.BlockSpec(summed.shape, lambda s, g: (0, 0))],
            out_specs=[pl.BlockSpec((rows // steps, block), lambda s, g: (s, 0))] * parts,
            scratch_shapes=[
                pltpu.VMEM((block, channels), jnp.float32),
                pltpu.VMEM((one, 2, block, block), jnp.float32),
            ],
        ),
        out_shape=[pltpu.HBM((rows, block), jnp.bfloat16)] * parts,
        compiler_params=pltpu.CompilerParams(vmem_limit_bytes=VMEM_LIMIT),
        cost_estimate=COST,
        name="cross_next",
    )(group_index, unit, raw, summed)


def turn(load, pieces, piece_rows, held_ref, base, width, rows, block):
    chunk = 16 * rows
    at = iota((chunk, chunk), 0)
    matrix = (iota((chunk, chunk), 1) == (at & 15) * rows + (at >> 4)).astype(jnp.bfloat16)
    total = pieces * piece_rows
    for c in range(-(-total // chunk)):
        begin, end = c * chunk, min((c + 1) * chunk, total)
        found = []
        for p in range(begin // piece_rows, (end - 1) // piece_rows + 1):
            low, high = max(begin, p * piece_rows), min(end, (p + 1) * piece_rows)
            found.append(load(p, low - p * piece_rows, high - low))
        piece = found[0] if len(found) == 1 else jnp.concatenate(found, axis=0)
        turned = jnp.dot(matrix[:, : end - begin], piece, preferred_element_type=jnp.float32).astype(jnp.bfloat16)
        for i in range(rows):
            held_ref[base + c * 16 : base + (c + 1) * 16, i * block : (i + 1) * block] = turned[i * 16 : (i + 1) * 16]
    used = -(-total // chunk) * 16
    if used < width:
        held_ref[base + used : base + width, :] = jnp.zeros((width - used, rows * block), jnp.bfloat16)


def mean_exp(corr, factor):
    return jnp.sum(jnp.exp(factor * corr), axis=0, keepdims=True) * (1.0 / corr.shape[0])


def own_kernel(factor, group_ref, terms_ref, trig_ref, out_ref, held_ref):
    parts, size, block = terms_ref.shape
    rows = out_ref.shape[0]
    sources = [lax.rem(group_ref[0] + (parts - p), parts) for p in range(parts)]

    def load(p, begin, count):
        return terms_ref[sources[p], begin : begin + count, :]

    half = parts // 2
    width = trig_ref.shape[1] // 2
    for h in range(2):
        turn(lambda p, *where: load(h * half + p, *where), half, size, held_ref, h * width, width, rows, block)
    for i in range(0, rows, 2):
        corr = jnp.dot(trig_ref[...], held_ref[:, i * block : (i + 2) * block], preferred_element_type=jnp.float32)
        mean = mean_exp(corr, factor)
        out_ref[i : i + 1, :] = mean[:, :block]
        out_ref[i + 1 : i + 2, :] = mean[:, block:]
    at = iota((rows, block), 0) + rows * group_ref[0]
    gap = (iota((rows, block), 1) - at) & (block - 1)
    out_ref[...] = jnp.where(gap == 0, 0.0, out_ref[...])


def own_part(group_index, terms, trig, factor):
    parts, _, block = terms.shape
    rows = block // 2 // parts
    return pl.pallas_call(
        functools.partial(own_kernel, factor),
        in_specs=[pl.BlockSpec(memory_space=pltpu.SMEM)] + [pl.BlockSpec(memory_space=pltpu.VMEM)] * 2,
        out_specs=pl.BlockSpec(memory_space=pltpu.VMEM),
        out_shape=jax.ShapeDtypeStruct((rows, block), jnp.float32),
        scratch_shapes=[pltpu.VMEM((trig.shape[1], rows * block), jnp.bfloat16)],
        compiler_params=pltpu.CompilerParams(vmem_limit_bytes=VMEM_LIMIT),
        name="own_part",
    )(group_index, terms, trig)


def first_kernel(trig_ref, *refs):
    *piece_refs, out_ref, held_ref = refs
    rows = 16
    size, block = piece_refs[0].shape
    width = held_ref.shape[0]
    turn(lambda p, b, n: piece_refs[p][b : b + n, :], len(piece_refs), size, held_ref, 0, width, rows, block)
    for i in range(0, rows, 2):
        cut = slice(i * block, (i + 2) * block)
        out_ref[:, cut] = jnp.dot(trig_ref[:, :width], held_ref[:, cut], preferred_element_type=jnp.float32)


def first_part(pieces, trig):
    rows = 16
    block = pieces[0].shape[1]
    return pl.pallas_call(
        first_kernel,
        in_specs=[pl.BlockSpec(memory_space=pltpu.VMEM)] * (1 + len(pieces)),
        out_specs=pl.BlockSpec(memory_space=pltpu.VMEM),
        out_shape=jax.ShapeDtypeStruct((trig.shape[0], rows * block), jnp.float32),
        scratch_shapes=[pltpu.VMEM((trig.shape[1] // 2, rows * block), jnp.bfloat16)],
        compiler_params=pltpu.CompilerParams(vmem_limit_bytes=VMEM_LIMIT),
        name="first_part",
    )(trig, *pieces)


def next_kernel(factor, group_ref, trig_ref, own_ref, summed_ref, share_ref, *refs):
    *piece_refs, out_ref, held_ref, wide_ref = refs
    rows = 16
    size, block = piece_refs[0].shape
    half = block // 2
    group = group_ref[0]
    width = held_ref.shape[0]
    turn(lambda p, b, n: piece_refs[p][b : b + n, :], len(piece_refs), size, held_ref, 0, width, rows, block)
    for i in range(0, rows, 2):
        cut = slice(i * block, (i + 2) * block)
        corr = jnp.dot(trig_ref[:, width:], held_ref[:, cut], preferred_element_type=jnp.float32)
        mean = mean_exp(share_ref[:, cut] + corr, factor)
        out_ref[i : i + 1, :] = mean[:, :block]
        out_ref[i + 1 : i + 2, :] = mean[:, block:]
    own = own_ref[...]
    at = iota((8, block), 0) + 8 * group
    gap = (iota((8, block), 1) - at) & (block - 1)
    top = (gap >= 1) & (gap <= half)
    upper, lower = jnp.where(top, own, 0.0), jnp.where(top, 0.0, own)
    wide_ref[...] = jnp.zeros_like(wide_ref)
    wide_ref[pl.ds(pl.multiple_of(rows * group, rows), rows), :] = out_ref[0:rows, :]
    own_at = pl.multiple_of(8 * group, 8)
    wide_ref[pl.ds(block + own_at, 8), :] = upper
    wide_ref[pl.ds(block + half + own_at, 8), :] = lower
    ones = jnp.ones((8, block), jnp.float32)
    by_row = dot(ones, wide_ref[...], ((1,), (1,)))
    degree = by_row[0:1, :block] + by_row[0:1, block:] + jnp.sum(own, axis=0, keepdims=True)
    out_ref[rows : rows + 8, :] = jnp.zeros((8, block), jnp.float32)
    out_ref[rows : rows + 1, :] = degree
    out_ref[rows + 1 : rows + 2, :] = jnp.sum(out_ref[0:rows, :], axis=0, keepdims=True)
    out_ref[rows + 8 :, :] = summed_ref[8:, :]


def next_part(group_index, share, pieces, trig, own, summed, factor):
    rows = 16
    block = pieces[0].shape[1]
    return pl.pallas_call(
        functools.partial(next_kernel, factor),
        in_specs=[pl.BlockSpec(memory_space=pltpu.SMEM)]
        + [pl.BlockSpec(memory_space=pltpu.VMEM)] * (4 + len(pieces)),
        out_specs=pl.BlockSpec(memory_space=pltpu.VMEM),
        out_shape=jax.ShapeDtypeStruct((rows + summed.shape[0], block), jnp.float32),
        scratch_shapes=[
            pltpu.VMEM((trig.shape[1] // 2, rows * block), jnp.bfloat16),
            pltpu.VMEM((2 * block, block), jnp.float32),
        ],
        compiler_params=pltpu.CompilerParams(vmem_limit_bytes=VMEM_LIMIT),
        name="next_part",
    )(group_index, trig, own, summed, share, *pieces)


def image_kernel(group_ref, parts_ref, before_ref, here_ref, after_ref, out_ref, own_ref, full_ref):
    groups, _, block = parts_ref.shape
    half = block // 2
    shares = parts_ref[0, 40:48, :]
    for s in range(groups):
        if s:
            shares = shares + parts_ref[s, 40:48, :]
        full_ref[0, 16 * s : 16 * s + 16, :] = parts_ref[s, 0:16, :]
        full_ref[1, 16 * s : 16 * s + 16, :] = parts_ref[s, 16:32, :]
        full_ref[2, 8 * s : 8 * s + 8, :] = parts_ref[s, 32:40, :]
    top = upper_half(half, block)
    own = full_ref[2, 0:half, :]
    full_ref[2, 0:half, :] = jnp.where(top, own, 0.0)
    full_ref[2, half:block, :] = jnp.where(top, 0.0, own)
    inv_root = lax.rsqrt(shares)
    scaled_before = before_ref[24:, :] * inv_root[0:1, :]
    scaled_own = here_ref[8:, :] * inv_root[1:2, :]
    scaled_after = after_ref[8:, :] * inv_root[2:3, :]
    along, across = ((1,), (1,)), ((1,), (0,))
    product = dot(scaled_own, full_ref[2], along) + dot(scaled_own, full_ref[2], across)
    product = product + dot(scaled_after, full_ref[0], along) + dot(scaled_before, full_ref[1], across)
    image = product * inv_root[1:2, :] * (3.0 * block)
    degree = shares[1:2, :]
    root_degree = jnp.sqrt(degree)
    degree_sum = jnp.sum(degree, axis=1, keepdims=True)
    proj = jnp.sum(root_degree * image, axis=1, keepdims=True)
    rest = image - root_degree * (proj / degree_sum)
    rest_sq = jnp.sum(rest * rest, axis=1, keepdims=True)
    count = image.shape[0]
    at, lane = iota((count, block), 0), iota((count, block), 1)
    stats = jnp.where(lane == at, proj, 0.0) + jnp.where(lane == at + count, rest_sq, 0.0)
    stats = jnp.sum(stats, axis=0, keepdims=True)
    stats = jnp.where(iota((1, block), 1) == 2 * count, degree_sum, stats)
    out_ref[...] = jnp.broadcast_to(stats, out_ref.shape)
    place = (lane == at + count * group_ref[0]).astype(jnp.float32)
    own_ref[0] = dot(place, image, along)
    own_ref[1] = dot(place, jnp.broadcast_to(root_degree, image.shape), along)


def image_part(group_index, parts, before, here, after, n_blk):
    groups, _, block = parts.shape
    count = here.shape[0] - 8
    return pl.pallas_call(
        image_kernel,
        in_specs=[pl.BlockSpec(memory_space=pltpu.SMEM)] + [pl.BlockSpec(memory_space=pltpu.VMEM)] * 4,
        out_specs=[pl.BlockSpec(memory_space=pltpu.VMEM)] * 2,
        out_shape=[
            jax.ShapeDtypeStruct((n_blk, block), jnp.float32),
            jax.ShapeDtypeStruct((2, count, count), jnp.float32),
        ],
        scratch_shapes=[pltpu.VMEM((3, block, block), jnp.float32)],
        compiler_params=pltpu.CompilerParams(vmem_limit_bytes=VMEM_LIMIT),
        name="image_part",
    )(group_index, parts, before, here, after)


def final_kernel(total_rows, stats_ref, own_ref, out_ref):
    count = out_ref.shape[1]
    stats = stats_ref[...]
    proj, rest_sq, degree = stats[:, :count], stats[:, count : 2 * count], stats[:, 2 * count : 2 * count + 1]
    ratio = jnp.sum(proj, axis=0, keepdims=True) / jnp.sum(degree, axis=0, keepdims=True)
    shift = proj / degree - ratio
    column_sq = jnp.sum(rest_sq + degree * (shift * shift), axis=0, keepdims=True)
    deflated = own_ref[0] - own_ref[1] * ratio
    out_ref[...] = deflated * lax.rsqrt(column_sq / total_rows + epsilon)


def final_part(stats, own, total_rows):
    count = own.shape[1]
    return pl.pallas_call(
        functools.partial(final_kernel, total_rows),
        in_specs=[pl.BlockSpec(memory_space=pltpu.VMEM)] * 2,
        out_specs=pl.BlockSpec(memory_space=pltpu.VMEM),
        out_shape=jax.ShapeDtypeStruct((count, count), jnp.float32),
        name="final_part",
    )(stats, own)


def per_device(coeffs, vectors):
    block, freq_local, channels = coeffs.shape
    group_size = lax.axis_size("grp")
    n_blk = lax.axis_size("blk")
    group_index = lax.axis_index("grp").astype(jnp.int32)[None]
    angles = freq_local * group_size
    factor = sharpness / math.sqrt(angles * channels)
    trig = trig_columns(freq_local, group_size, group_index[0])

    begun, by_freq = start(group_index, coeffs.transpose(1, 0, 2), vectors, group_size)
    summed = jnp.sum(lax.all_to_all(begun, "grp", 0, 0, tiled=True), axis=0)
    after_raw = passed_along(by_freq, "blk", -1)
    summed_after = passed_along(summed, "blk", -1)
    own_terms, own_unit = cross_own(by_freq, summed, group_size, 9)
    own_terms = lax.all_to_all(own_terms, "grp", 0, 0, tiled=True)
    next_terms = cross_next(group_index, own_unit, after_raw, summed_after, group_size, 9)
    next_terms = [next_terms[0]] + [passed_along(next_terms[r], "grp", r) for r in range(1, group_size)]
    own_aff = own_part(group_index, own_terms, trig, factor)
    share = first_part(next_terms[: group_size // 2], trig)
    found = next_part(group_index, share, next_terms[group_size // 2 :], trig, own_aff, summed, factor)

    found_before = passed_along(found, "blk", 1)
    edge_after = passed_along(found[16:24], "blk", -1)
    edge_before = passed_along(found[16:24], "blk", 2)
    zeros = jnp.zeros((5, block), jnp.float32)
    shares = jnp.concatenate(
        [
            found_before[16:17] + edge_before[1:2],
            found[16:17] + found_before[17:18],
            edge_after[0:1] + found[17:18],
            zeros,
        ],
        axis=0,
    )
    sent = jnp.concatenate([found[:16], found_before[:16], own_aff, shares], axis=0)
    sent = jnp.broadcast_to(sent[None], (group_size,) + sent.shape)
    parts = lax.all_to_all(sent, "grp", 0, 0, tiled=True)
    stats, own = image_part(group_index, parts, found_before, summed, summed_after, n_blk)
    stats = lax.all_to_all(stats, "blk", 0, 0, tiled=True)
    return final_part(stats, own, block * n_blk)


def solution(mesh):
    placed = (P("blk", "grp", None), P(("blk", "grp"), None))
    return jax.shard_map(
        per_device, mesh=mesh, in_specs=placed, out_specs=P(("blk", "grp"), None), check_vma=False
    )
```
